32 devices in a mesh: section: 4 (over y, x), tensor: 8 (over z, core).
Axes of the slice: x: 2, y: 2, z: 4, core: 2. Of those that a mesh axis runs over, the one named last changes fastest.
Arguments:
- inputs: bfloat16 [4, 1024, 8192], P('section', None, 'tensor'), may hold values from -6 to 6
- preact: bfloat16 [4, 1024, 32768], P('section', None, 'tensor'), may hold values from -6 to 6
- handoff: bfloat16 [4, 1024, 8192], P('section', None, 'tensor'), may hold values from -6 to 6
- first_blocks: bfloat16 [4, 128, 6, 256, 256], P('section', 'tensor'), may hold values from -0.15625 to 0.15625
- second_blocks: bfloat16 [4, 128, 6, 256, 256], P('section', 'tensor'), may hold values from -0.078125 to 0.078125
- left_one: bfloat16 [4, 8192, 256], P('section', 'tensor'), may hold values from -0.0625 to 0.0625
- right_one: bfloat16 [4, 256, 32768], P('section', None, 'tensor'), may hold values from -0.375 to 0.375
- left_two: bfloat16 [4, 32768, 256], P('section', 'tensor'), may hold values from -0.03125 to 0.03125
- right_two: bfloat16 [4, 256, 8192], P('section', None, 'tensor'), may hold values from -0.375 to 0.375
Outputs:
- input_grad: bfloat16 [4, 1024, 8192], P('section', None, 'tensor')
- first_grad: bfloat16 [4, 128, 6, 256, 256], P('section', 'tensor')
- second_grad: bfloat16 [4, 128, 6, 256, 256], P('section', 'tensor')
- leftone_grad: bfloat16 [4, 8192, 256], P('section', 'tensor')
- rightone_grad: bfloat16 [4, 256, 32768], P('section', None, 'tensor')
- lefttwo_grad: bfloat16 [4, 32768, 256], P('section', 'tensor')
- righttwo_grad: bfloat16 [4, 256, 8192], P('section', None, 'tensor')
The draws below stay inside these ranges and needn't reach their ends.
All inputs are finite; a program needn't handle non-finite values.
Results may differ from the reference program's by a relative error of at most 0.0061.
Values may be sent and summed in bfloat16 or wider, within the bound.
No kernel may reach another device: no remote copies, remote signals or barrier semaphores. Data moves between devices by JAX's collectives and lax.ppermute only.
A program may use at most 256 MiB of HBM per device.

```python
import jax
import jax.numpy as jnp
import numpy as np

D = 8192
FF = 32768
BLOCK = 256
RANK = 256
LEVELS = 5
TOKENS = 1024
SECTIONS = 4
LINKS = 6
IN_BLOCKS = 32
HID_BLOCKS = 128
GROUP = 4


def steps_of(rng, dims, pieces, smallest, largest):
    gain, own = 1.0, jax.random.fold_in(rng, 6)
    for dim, blocks in pieces:
        heights = jnp.exp(jax.random.uniform(jax.random.fold_in(own, dim), (blocks,), jnp.float32, smallest / len(pieces), largest / len(pieces)))
        gain = gain * jnp.repeat(heights, dims[dim] // blocks).reshape([-1 if axis == dim else 1 for axis in range(len(dims))])
    return gain


def bell_draw(key, shape, scale, reach, pieces=(), kind=jnp.bfloat16):
    array = scale * jax.random.normal(key, shape, jnp.float32)
    if pieces:
        array = array * steps_of(key, shape, pieces, -0.22, 0.18)
    return jnp.clip(array, -reach, reach).astype(kind)


def setup_inputs(seed: int = 0) -> dict:
    arg_keys = jax.random.split(jax.random.key(seed), 10)
    return {
        "inputs": bell_draw(arg_keys[0], (SECTIONS, TOKENS, D), 1.0, 6.0, ((0, 4), (2, 8))),
        "preact": bell_draw(arg_keys[1], (SECTIONS, TOKENS, FF), 1.0, 6.0, ((0, 4), (2, 8))),
        "handoff": bell_draw(arg_keys[2], (SECTIONS, TOKENS, D), 1.0, 6.0, ((0, 4), (2, 8))),
        "first_blocks": bell_draw(arg_keys[3], (SECTIONS, HID_BLOCKS, LINKS, BLOCK, BLOCK), (LINKS * BLOCK) ** -0.5, 0.15625, ((0, 4), (1, 8))),
        "second_blocks": bell_draw(arg_keys[4], (SECTIONS, HID_BLOCKS, LINKS, BLOCK, BLOCK), (LINKS * GROUP * BLOCK) ** -0.5, 0.078125, ((0, 4), (1, 8))),
        "left_one": bell_draw(arg_keys[5], (SECTIONS, D, RANK), D ** -0.5, 0.0625, ((0, 4), (1, 8))),
        "right_one": bell_draw(arg_keys[6], (SECTIONS, RANK, FF), RANK ** -0.5, 0.375, ((0, 4), (2, 8))),
        "left_two": bell_draw(arg_keys[7], (SECTIONS, FF, RANK), FF ** -0.5, 0.03125, ((0, 4), (1, 8))),
        "right_two": bell_draw(arg_keys[8], (SECTIONS, RANK, D), RANK ** -0.5, 0.375, ((0, 4), (2, 8))),
    }


def gelu_pair(preact):
    values = preact.astype(jnp.float32)
    normal_cdf = 0.5 * (1.0 + jax.scipy.special.erf(values * 0.7071067811865476))
    density = jnp.exp(-0.5 * values * values) * 0.3989422804014327
    return values * normal_cdf, normal_cdf + values * density


def partner_table(count_in, degree):
    if degree == 0:
        return np.arange(count_in)
    return np.arange(count_in) ^ (1 << (degree - 1))


def one_section(inputs, preact, upstream, first_blocks, second_blocks, left_one, right_one, left_two, right_two):
    token_count = inputs.shape[0]
    link_count = LEVELS + 1
    home_block = np.arange(HID_BLOCKS) // GROUP
    activated, slope_vals = gelu_pair(preact)
    activated = activated.astype(jnp.bfloat16)
    proj_in = jnp.dot(inputs, left_one, preferred_element_type=jnp.float32).astype(jnp.bfloat16)
    proj_act = jnp.dot(activated, left_two, preferred_element_type=jnp.float32).astype(jnp.bfloat16)
    proj_grad = jnp.dot(upstream, right_two.T, preferred_element_type=jnp.float32).astype(jnp.bfloat16)
    grad_act = jnp.dot(proj_grad, left_two.T, preferred_element_type=jnp.float32).reshape(token_count, HID_BLOCKS, BLOCK)
    up_blocks = upstream.astype(jnp.float32).reshape(token_count, IN_BLOCKS, BLOCK)
    in_blocks = inputs.astype(jnp.float32).reshape(token_count, IN_BLOCKS, BLOCK)
    for degree in range(link_count):
        link_table = partner_table(IN_BLOCKS, degree)[home_block]
        grad_act = grad_act + jnp.einsum('tib,ieb->tie', up_blocks[:, link_table], second_blocks[:, degree].astype(jnp.float32))
    hidden_grad = (grad_act.reshape(token_count, FF) * slope_vals).astype(jnp.bfloat16)
    back_rank = jnp.dot(hidden_grad, right_one.T, preferred_element_type=jnp.float32).astype(jnp.bfloat16)
    hid_blocks = hidden_grad.astype(jnp.float32).reshape(token_count, HID_BLOCKS, BLOCK)
    act_blocks = activated.astype(jnp.float32).reshape(token_count, HID_BLOCKS, BLOCK)
    summed_grad = jnp.dot(back_rank, left_one.T, preferred_element_type=jnp.float32).reshape(token_count, IN_BLOCKS, BLOCK)
    first_list = []
    second_list = []
    for degree in range(link_count):
        partner = partner_table(IN_BLOCKS, degree)
        link_table = partner[home_block]
        partial_value = jnp.einsum('tie,ibe->tib', hid_blocks, first_blocks[:, degree].astype(jnp.float32))
        grouped = partial_value.reshape(token_count, IN_BLOCKS, GROUP, BLOCK).sum(axis=2)
        summed_grad = summed_grad + grouped[:, partner]
        first_list.append(jnp.einsum('tib,tie->ibe', in_blocks[:, link_table], hid_blocks).astype(jnp.bfloat16))
        second_list.append(jnp.einsum('tie,tib->ieb', act_blocks, up_blocks[:, link_table]).astype(jnp.bfloat16))
    input_grad = summed_grad.reshape(token_count, D).astype(jnp.bfloat16)
    first_grad = jnp.stack(first_list, axis=1)
    second_grad = jnp.stack(second_list, axis=1)
    leftone_grad = jnp.dot(inputs.T, back_rank, preferred_element_type=jnp.float32).astype(jnp.bfloat16)
    rightone_grad = jnp.dot(proj_in.T, hidden_grad, preferred_element_type=jnp.float32).astype(jnp.bfloat16)
    lefttwo_grad = jnp.dot(activated.T, proj_grad, preferred_element_type=jnp.float32).astype(jnp.bfloat16)
    righttwo_grad = jnp.dot(proj_act.T, upstream, preferred_element_type=jnp.float32).astype(jnp.bfloat16)
    return (input_grad, first_grad, second_grad, leftone_grad, rightone_grad, lefttwo_grad, righttwo_grad)


def reference(inputs, preact, handoff, first_blocks, second_blocks, left_one, right_one, left_two, right_two):
    collected = []
    for section_pos in range(SECTIONS):
        collected.append(one_section(inputs[section_pos], preact[section_pos], handoff[(section_pos + 1) % SECTIONS],
                                   first_blocks[section_pos], second_blocks[section_pos], left_one[section_pos],
                                   right_one[section_pos], left_two[section_pos], right_two[section_pos]))
    stacked = [jnp.stack([member[number] for member in collected]) for number in range(7)]
    return (stacked[0], stacked[1], stacked[2], stacked[3], stacked[4], stacked[5], stacked[6])
```

```python
import functools

import jax
import jax.numpy as jnp
from jax import lax
from jax.experimental import pallas as pl
from jax.experimental.pallas import tpu as pltpu
from jax.sharding import PartitionSpec as P

CHUNKS = 2
BF16 = jnp.bfloat16
F32 = jnp.float32


def swapped(value, bit):
    pairs = [(source, source ^ (1 << bit)) for source in range(lax.axis_size("tensor"))]
    return lax.ppermute(value, "tensor", pairs)


def shifted(value):
    peers = lax.axis_size("section")
    return lax.ppermute(value, "section", [(i, (i - 1) % peers) for i in range(peers)])


def tree_sum(value):
    bits = lax.axis_size("tensor").bit_length() - 1
    place = lax.axis_index("tensor")
    for bit in range(bits - 1):
        half = value.shape[0] // 2
        mine = (place >> bit) & 1
        keep = lax.dynamic_slice_in_dim(value, mine * half, half)
        give = lax.dynamic_slice_in_dim(value, (1 - mine) * half, half)
        value = keep + swapped(give.astype(BF16), bit).astype(F32)
    value = (value + swapped(value.astype(BF16), bits - 1).astype(F32)).astype(BF16)
    for bit in reversed(range(bits - 1)):
        mine = (place >> bit) & 1
        other = swapped(value, bit)
        first = jnp.where(mine == 0, value, other)
        second = jnp.where(mine == 0, other, value)
        value = jnp.concatenate([first, second])
    return value


def nt(left, right):
    return lax.dot_general(left, right, (((1,), (1,)), ((), ())), preferred_element_type=F32)


def nn(left, right):
    return jnp.dot(left, right, preferred_element_type=F32)


def wide(parts):
    return parts[0] if len(parts) == 1 else jnp.concatenate(parts, axis=1)


def slope_of(values):
    normal_cdf = 0.5 * (1.0 + lax.erf(values * 0.7071067811865476))
    density = jnp.exp(-0.5 * values * values) * 0.3989422804014327
    return normal_cdf + values * density


def params(flops, moved, steps):
    return dict(
        cost_estimate=pl.CostEstimate(flops=flops, bytes_accessed=moved, transcendentals=0),
        compiler_params=pltpu.CompilerParams(
            dimension_semantics=("arbitrary",) * steps, vmem_limit_bytes=56 * 2**20
        ),
    )


def hidden_kernel(links, late, group, *refs):
    ups, refs = refs[:links], refs[links:]
    proj, refs = refs[0], refs[1:]
    seconds, refs = refs[:links], refs[links:]
    left_two, preact, right_one, refs = refs[0], refs[1], refs[2], refs[3:]
    firsts, refs = refs[:late], refs[late:]
    hidden, refs = refs[0], refs[1:]
    parts, refs = refs[:late], refs[late:]
    rank, up_all, hid_all = refs
    c, j = pl.program_id(0), pl.program_id(1)
    size = hidden.shape[1]

    @pl.when(j == 0)
    def _():
        for k in range(links):
            up_all[:, k * size : (k + 1) * size] = ups[k][...]
        up_all[:, links * size :] = proj[...]

    weights = wide([ref[...] for ref in seconds] + [left_two[...]])
    grad = nt(up_all[...], weights)
    hid = (grad * slope_of(preact[...].astype(F32))).astype(BF16)
    hidden[...] = hid
    hid_all[:, pl.ds(pl.multiple_of(j * size, size), size)] = hid

    @pl.when(j == group - 1)
    def _():
        group_grad = hid_all[...]
        for ref, part in zip(firsts, parts):
            part[...] = nt(group_grad, wide([ref[g] for g in range(group)])).astype(BF16)
        term = nt(group_grad, right_one[...])

        @pl.when(c == 0)
        def _():
            rank[...] = term

        @pl.when(c > 0)
        def _():
            rank[...] += term


def hidden_call(ups, flips, proj, second, left_two, preact, right_one, first, late_from, chunk):
    rows = ups[0].shape[0]
    _, hid_count, links, size, _ = first.shape
    count_in = ups[0].shape[1] // size
    group = hid_count // count_in
    rank = proj.shape[1]
    late = links - late_from
    in_specs = [
        pl.BlockSpec((rows, size), lambda c, j, flip=flip: (0, c ^ flip)) for flip in flips
    ]
    in_specs.append(pl.BlockSpec((rows, rank), lambda c, j: (chunk, 0)))
    in_specs += [
        pl.BlockSpec((None, None, None, size, size), lambda c, j, k=k: (0, c * group + j, k, 0, 0))
        for k in range(links)
    ]
    in_specs.append(pl.BlockSpec((None, size, rank), lambda c, j: (0, c * group + j, 0)))
    in_specs.append(pl.BlockSpec((None, rows, size), lambda c, j: (0, chunk, c * group + j)))
    in_specs.append(pl.BlockSpec((None, rank, group * size), lambda c, j: (0, 0, c)))
    in_specs += [
        pl.BlockSpec((None, group, None, size, size), lambda c, j, k=k: (0, c, k, 0, 0))
        for k in range(late_from, links)
    ]
    out_specs = [pl.BlockSpec((rows, size), lambda c, j: (0, c * group + j))]
    out_specs += [pl.BlockSpec((rows, size), lambda c, j: (0, c))] * late
    out_specs.append(pl.BlockSpec((rows, rank), lambda c, j: (0, 0)))
    width = hid_count * size
    out_shape = [jax.ShapeDtypeStruct((rows, width), BF16)]
    out_shape += [jax.ShapeDtypeStruct((rows, count_in * size), BF16)] * late
    out_shape.append(jax.ShapeDtypeStruct((rows, rank), F32))
    flops = 2 * rows * width * (size * links + rank * 2 + size * late)
    moved = 2 * width * (2 * rows + size * (links + late) + 2 * rank)
    return pl.pallas_call(
        functools.partial(hidden_kernel, links, late, group),
        grid=(count_in, group),
        in_specs=in_specs,
        out_specs=out_specs,
        out_shape=out_shape,
        scratch_shapes=[
            pltpu.VMEM((rows, links * size + rank), BF16),
            pltpu.VMEM((rows, group * size), BF16),
        ],
        name="hidden_grad",
        **params(flops, moved, 2),
    )(
        *ups, proj, *[second] * links, left_two, preact, right_one, *[first] * late
    )


def near_kernel(near, group, hid, *refs):
    weights, refs = refs[0], refs[1:]
    far_weights, rank, left_one, base, far, total = refs
    kk = pl.program_id(1)
    term = nt(hid[...], wide([weights[g] for g in range(group)]))

    @pl.when(kk == 0)
    def _():
        total[...] = term + nt(rank[...], left_one[...])
        far[...] = nt(hid[...], wide([far_weights[g] for g in range(group)])).astype(BF16)

    @pl.when(kk > 0)
    def _():
        total[...] += term

    @pl.when(kk == near - 1)
    def _():
        base[...] = total[...]


def near_call(hidden, first, rank, left_one, near, chunk):
    rows = hidden.shape[0]
    _, hid_count, links, size, _ = first.shape
    count_in = left_one.shape[1] // size
    group = hid_count // count_in
    ranks = rank.shape[1]

    def mate(c, kk):
        return c ^ ((1 << kk) >> 1)

    width = count_in * size
    return pl.pallas_call(
        functools.partial(near_kernel, near, group),
        grid=(count_in, near),
        in_specs=[
            pl.BlockSpec((rows, group * size), lambda c, kk: (0, mate(c, kk))),
            pl.BlockSpec(
                (None, group, None, size, size), lambda c, kk: (0, mate(c, kk), kk, 0, 0)
            ),
            pl.BlockSpec((None, group, None, size, size), lambda c, kk: (0, c, near, 0, 0)),
            pl.BlockSpec((rows, ranks), lambda c, kk: (chunk, 0)),
            pl.BlockSpec((None, size, ranks), lambda c, kk: (0, c, 0)),
        ],
        out_specs=[
            pl.BlockSpec((rows, size), lambda c, kk: (0, c)),
            pl.BlockSpec((rows, size), lambda c, kk: (0, c)),
        ],
        out_shape=[
            jax.ShapeDtypeStruct((rows, width), F32),
            jax.ShapeDtypeStruct((rows, width), BF16),
        ],
        scratch_shapes=[pltpu.VMEM((rows, size), F32)],
        name="near_parts",
        **params(
            2 * rows * width * (group * size * (near + 1) + ranks),
            2 * hid_count * size * (size * (near + 1) + rows * near) + 6 * rows * width,
            2,
        ),
    )(hidden, first, first, rank, left_one)


def second_kernel(links, chunks, rows, *refs):
    ups, refs = refs[: links * chunks], refs[links * chunks :]
    proj, act, out, left_two, up_all = refs
    size = act.shape[1]

    @pl.when(pl.program_id(1) == 0)
    def _():
        for m in range(chunks):
            for k in range(links):
                up_all[m * rows : (m + 1) * rows, k * size : (k + 1) * size] = ups[m * links + k][
                    ...
                ]
        up_all[:, links * size :] = proj[...]

    grads = nn(act[...].T, up_all[...]).astype(BF16)
    for k in range(links):
        out[k] = grads[:, k * size : (k + 1) * size]
    left_two[...] = grads[:, links * size :]


def second_call(ups, flips, proj, act, shape):
    chunks = len(ups)
    rows = ups[0][0].shape[0]
    tokens = rows * chunks
    _, hid_count, links, size, _ = shape
    count_in = ups[0][0].shape[1] // size
    group = hid_count // count_in
    rank = proj.shape[1]
    in_specs = [
        pl.BlockSpec((rows, size), lambda c, j, flip=flip: (0, c ^ flip))
        for _ in range(chunks)
        for flip in flips
    ]
    in_specs.append(pl.BlockSpec((tokens, rank), lambda c, j: (0, 0)))
    in_specs.append(pl.BlockSpec((tokens, size), lambda c, j: (0, c * group + j)))
    width = hid_count * size
    return pl.pallas_call(
        functools.partial(second_kernel, links, chunks, rows),
        grid=(count_in, group),
        in_specs=in_specs,
        out_specs=[
            pl.BlockSpec(
                (None, None, links, size, size), lambda c, j: (0, c * group + j, 0, 0, 0)
            ),
            pl.BlockSpec((None, size, rank), lambda c, j: (0, c * group + j, 0)),
        ],
        out_shape=[
            jax.ShapeDtypeStruct(shape, BF16),
            jax.ShapeDtypeStruct((1, width, rank), BF16),
        ],
        scratch_shapes=[pltpu.VMEM((tokens, links * size + rank), BF16)],
        name="second_grad",
        **params(
            2 * tokens * width * (links * size + rank),
            2 * width * (tokens + links * size + rank),
            2,
        ),
    )(*[up for chunk in ups for up in chunk], proj, act)


def first_kernel(links, chunks, rows, *refs):
    ins, refs = refs[: links * chunks], refs[links * chunks :]
    proj, refs = refs[0], refs[1:]
    hids, refs = refs[:chunks], refs[chunks:]
    out, right_one, in_all = refs
    size = hids[0].shape[1]

    @pl.when(pl.program_id(1) == 0)
    def _():
        for m in range(chunks):
            for k in range(links):
                in_all[k * size : (k + 1) * size, m * rows : (m + 1) * rows] = ins[m * links + k][
                    ...
                ].T
        in_all[links * size :, :] = proj[...].T

    hid = jnp.concatenate([ref[...] for ref in hids], axis=0)
    grads = nn(in_all[...], hid).astype(BF16)
    for k in range(links):
        out[k] = grads[k * size : (k + 1) * size]
    right_one[...] = grads[links * size :]


def first_call(ins, flips, proj, hids, shape):
    chunks = len(ins)
    rows = ins[0][0].shape[0]
    tokens = rows * chunks
    _, hid_count, links, size, _ = shape
    count_in = ins[0][0].shape[1] // size
    group = hid_count // count_in
    rank = proj.shape[1]
    in_specs = [
        pl.BlockSpec((rows, size), lambda c, j, flip=flip: (0, c ^ flip))
        for _ in range(chunks)
        for flip in flips
    ]
    in_specs.append(pl.BlockSpec((tokens, rank), lambda c, j: (0, 0)))
    in_specs += [pl.BlockSpec((rows, size), lambda c, j: (0, c * group + j))] * chunks
    width = hid_count * size
    return pl.pallas_call(
        functools.partial(first_kernel, links, chunks, rows),
        grid=(count_in, group),
        in_specs=in_specs,
        out_specs=[
            pl.BlockSpec(
                (None, None, links, size, size), lambda c, j: (0, c * group + j, 0, 0, 0)
            ),
            pl.BlockSpec((None, rank, size), lambda c, j: (0, 0, c * group + j)),
        ],
        out_shape=[
            jax.ShapeDtypeStruct(shape, BF16),
            jax.ShapeDtypeStruct((1, rank, width), BF16),
        ],
        scratch_shapes=[pltpu.VMEM((links * size + rank, tokens), BF16)],
        name="first_grad",
        **params(
            2 * tokens * width * (links * size + rank),
            2 * width * (tokens + links * size + rank),
            2,
        ),
    )(*[value for chunk in ins for value in chunk], proj, *hids)


def body(
    inputs, preact, handoff, first_blocks, second_blocks, left_one, right_one, left_two, right_two
):
    shape = first_blocks.shape
    links, size = shape[2], shape[-1]
    tokens, feats = inputs.shape[1:]
    count_in = feats // size
    near = count_in.bit_length()
    flips = [(1 << k) >> 1 if k < near else 0 for k in range(links)]
    rows = tokens // CHUNKS
    spans = [slice(m * rows, (m + 1) * rows) for m in range(CHUNKS)]

    def spread(value):
        return [value] * near + [swapped(value, k - near) for k in range(near, links)]

    upstream = [shifted(handoff[0, span]) for span in spans]
    in_parts = [inputs[0, span] for span in spans]
    in_sets = [spread(in_parts[0])]
    up_sets = [spread(value) for value in upstream]
    for m in range(1, CHUNKS):
        value, _ = lax.optimization_barrier((in_parts[m], up_sets[m - 1][-1]))
        sets = spread(value)
        in_sets.append([in_parts[m]] * near + sets[near:])

    values = preact[0].astype(F32)
    act = (values * (0.5 * (1.0 + lax.erf(values * 0.7071067811865476)))).astype(BF16)
    early = jnp.concatenate([nn(inputs[0], left_one[0]), nn(act, left_two[0])], axis=1)
    early = tree_sum(early)
    ranks = left_one.shape[2]
    proj_in, proj_act = early[:, :ranks], early[:, ranks:]
    proj_grad = tree_sum(
        jnp.concatenate([nt(value, right_two[0]) for value in upstream], axis=0)
    )

    hids, far, back = [], [], []
    for m in range(CHUNKS):
        hid, *parts, rank = hidden_call(
            up_sets[m],
            flips,
            proj_grad,
            second_blocks,
            left_two,
            preact,
            right_one,
            first_blocks,
            near + 1,
            m,
        )
        hids.append(hid)
        back.append(rank)
        far.append([swapped(part, k + 1) for k, part in enumerate(parts)])
    back_rank = tree_sum(jnp.concatenate(back, axis=0))

    second_grad, lefttwo_grad = second_call(up_sets, flips, proj_grad, act, shape)
    first_grad, rightone_grad = first_call(in_sets, flips, proj_in, hids, shape)
    leftone_grad = nn(inputs[0].T, back_rank).astype(BF16)[None]
    righttwo_grad = nn(proj_act.T, jnp.concatenate(upstream, axis=0)).astype(BF16)[None]
    input_grad = []
    for m in range(CHUNKS):
        base, beside = near_call(hids[m], first_blocks, back_rank, left_one, near, m)
        total = base + swapped(beside, 0).astype(F32)
        for part in far[m]:
            total = total + part.astype(F32)
        input_grad.append(total.astype(BF16))
    return (
        jnp.concatenate(input_grad, axis=0)[None],
        first_grad,
        second_grad,
        leftone_grad,
        rightone_grad,
        lefttwo_grad,
        righttwo_grad,
    )


def solution(mesh):
    by_feature = P("section", None, "tensor")
    by_block = P("section", "tensor", None, None, None)
    by_row = P("section", "tensor", None)
    in_specs = (
        by_feature,
        by_feature,
        by_feature,
        by_block,
        by_block,
        by_row,
        by_feature,
        by_row,
        by_feature,
    )
    out_specs = (
        by_feature,
        by_block,
        by_block,
        by_row,
        by_feature,
        by_row,
        by_feature,
    )
    return jax.shard_map(body, mesh=mesh, in_specs=in_specs, out_specs=out_specs, check_vma=False)
```

```python
import functools

import jax
import jax.numpy as jnp
from jax import lax
from jax.experimental import pallas as pl
from jax.experimental.pallas import tpu as pltpu
from jax.sharding import PartitionSpec as P

CHUNKS = 2
BF16 = jnp.bfloat16
F32 = jnp.float32


def swapped(value, bit):
    pairs = [(source, source ^ (1 << bit)) for source in range(lax.axis_size("tensor"))]
    return lax.ppermute(value, "tensor", pairs)


def shifted(value):
    peers = lax.axis_size("section")
    return lax.ppermute(value, "section", [(i, (i - 1) % peers) for i in range(peers)])


def tree_sum(value):
    bits = lax.axis_size("tensor").bit_length() - 1
    place = lax.axis_index("tensor")
    for bit in range(bits - 1):
        half = value.shape[0] // 2
        mine = (place >> bit) & 1
        keep = lax.dynamic_slice_in_dim(value, mine * half, half)
        give = lax.dynamic_slice_in_dim(value, (1 - mine) * half, half)
        give = give if bit == 0 else give.astype(BF16)
        value = keep + swapped(give, bit).astype(F32)
    value = (value + swapped(value.astype(BF16), bits - 1).astype(F32)).astype(BF16)
    for bit in reversed(range(bits - 1)):
        mine = (place >> bit) & 1
        other = swapped(value, bit)
        first = jnp.where(mine == 0, value, other)
        second = jnp.where(mine == 0, other, value)
        value = jnp.concatenate([first, second])
    return value


def nt(left, right):
    return lax.dot_general(left, right, (((1,), (1,)), ((), ())), preferred_element_type=F32)


def nn(left, right):
    return jnp.dot(left, right, preferred_element_type=F32)


def wide(parts):
    return parts[0] if len(parts) == 1 else jnp.concatenate(parts, axis=1)


def after(value, *others):
    return lax.optimization_barrier((value, *others))[0]


def gate_kernel(strip, preact, left_two, act, slope, proj):
    def one(r, _):
        rows = pl.ds(pl.multiple_of(r * strip, strip), strip)
        values = preact[rows, :].astype(F32)
        normal_cdf = 0.5 * (1.0 + lax.erf(values * 0.7071067811865476))
        density = jnp.exp(-0.5 * values * values) * 0.3989422804014327
        act[rows, :] = (values * normal_cdf).astype(BF16)
        slope[rows, :] = normal_cdf + values * density
        return 0

    lax.fori_loop(0, preact.shape[0] // strip, one, 0)
    term = nn(act[...], left_two[...])

    @pl.when(pl.program_id(0) == 0)
    def _():
        proj[...] = term

    @pl.when(pl.program_id(0) > 0)
    def _():
        proj[...] += term


def gate_call(preact, left_two, size):
    _, tokens, width = preact.shape
    rank = left_two.shape[2]
    return pl.pallas_call(
        functools.partial(gate_kernel, min(64, tokens)),
        grid=(width // size,),
        in_specs=[
            pl.BlockSpec((None, tokens, size), lambda i: (0, 0, i)),
            pl.BlockSpec((None, size, rank), lambda i: (0, i, 0)),
        ],
        out_specs=[
            pl.BlockSpec((tokens, size), lambda i: (0, i)),
            pl.BlockSpec((tokens, size), lambda i: (0, i)),
            pl.BlockSpec((tokens, rank), lambda i: (0, 0)),
        ],
        out_shape=[
            jax.ShapeDtypeStruct((tokens, width), BF16),
            jax.ShapeDtypeStruct((tokens, width), F32),
            jax.ShapeDtypeStruct((tokens, rank), F32),
        ],
        name="gate",
        **params(1),
    )(preact, left_two)


def params(steps):
    return dict(
        cost_estimate=pl.CostEstimate(flops=1024, bytes_accessed=1024, transcendentals=0),
        compiler_params=pltpu.CompilerParams(
            dimension_semantics=("arbitrary",) * steps, vmem_limit_bytes=56 * 2**20
        ),
    )


def hidden_kernel(links, late, group, *refs):
    ups, refs = refs[:links], refs[links:]
    proj, refs = refs[0], refs[1:]
    seconds, refs = refs[:links], refs[links:]
    left_two, slope, right_one, refs = refs[0], refs[1], refs[2], refs[3:]
    firsts, refs = refs[:late], refs[late:]
    hidden, refs = refs[0], refs[1:]
    parts, refs = refs[: late * CHUNKS], refs[late * CHUNKS :]
    rank, up_all, hid_all = refs
    c, j = pl.program_id(0), pl.program_id(1)
    size = hidden.shape[1]

    @pl.when(j == 0)
    def _():
        for k in range(links):
            up_all[:, k * size : (k + 1) * size] = ups[k][...]
        up_all[:, links * size :] = proj[...]

    weights = wide([ref[...] for ref in seconds] + [left_two[...]])
    grad = nt(up_all[...], weights)
    hid = (grad * slope[...]).astype(BF16)
    hidden[...] = hid
    hid_all[:, pl.ds(pl.multiple_of(j * size, size), size)] = hid

    @pl.when(j == group - 1)
    def _():
        group_grad = hid_all[...]
        for n, ref in enumerate(firsts):
            part = nt(group_grad, wide([ref[g] for g in range(group)])).astype(BF16)
            for m in range(CHUNKS):
                piece = parts[n * CHUNKS + m]
                piece[...] = part[m * piece.shape[0] : (m + 1) * piece.shape[0]]
        term = nt(group_grad, right_one[...])

        @pl.when(c == 0)
        def _():
            rank[...] = term

        @pl.when(c > 0)
        def _():
            rank[...] += term


def hidden_call(ups, flips, proj, second, left_two, slope, right_one, first, late_from, chunk):
    rows = ups[-1][0].shape[0]
    _, hid_count, links, size, _ = first.shape
    count_in = ups[0][0].shape[1] // size
    group = hid_count // count_in
    rank = proj.shape[1]
    late = links - late_from
    in_specs = [
        pl.BlockSpec((rows, size), lambda c, j, flip=flip, place=place: (place, c ^ flip))
        for (_, place), flip in zip(ups, flips)
    ]
    in_specs.append(pl.BlockSpec((rows, rank), lambda c, j: (chunk, 0)))
    in_specs += [
        pl.BlockSpec((None, None, None, size, size), lambda c, j, k=k: (0, c * group + j, k, 0, 0))
        for k in range(links)
    ]
    in_specs.append(pl.BlockSpec((None, size, rank), lambda c, j: (0, c * group + j, 0)))
    in_specs.append(pl.BlockSpec((rows, size), lambda c, j: (chunk, c * group + j)))
    in_specs.append(pl.BlockSpec((None, rank, group * size), lambda c, j: (0, 0, c)))
    in_specs += [
        pl.BlockSpec((None, group, None, size, size), lambda c, j, k=k: (0, c, k, 0, 0))
        for k in range(late_from, links)
    ]
    out_specs = [pl.BlockSpec((rows, size), lambda c, j: (0, c * group + j))]
    out_specs += [pl.BlockSpec((rows // CHUNKS, size), lambda c, j: (0, c))] * (late * CHUNKS)
    out_specs.append(pl.BlockSpec((rows, rank), lambda c, j: (0, 0)))
    width = hid_count * size
    out_shape = [jax.ShapeDtypeStruct((rows, width), BF16)]
    out_shape += [
        jax.ShapeDtypeStruct((rows // CHUNKS, count_in * size), BF16)
    ] * (late * CHUNKS)
    out_shape.append(jax.ShapeDtypeStruct((rows, rank), F32))
    return pl.pallas_call(
        functools.partial(hidden_kernel, links, late, group),
        grid=(count_in, group),
        in_specs=in_specs,
        out_specs=out_specs,
        out_shape=out_shape,
        scratch_shapes=[
            pltpu.VMEM((rows, links * size + rank), BF16),
            pltpu.VMEM((rows, group * size), BF16),
        ],
        name="hidden_grad",
        **params(2),
    )(
        *[up for up, _ in ups], proj, *[second] * links, left_two, slope, right_one, *[first] * late
    )


def near_kernel(near, group, hid, *refs):
    weights, refs = refs[0], refs[1:]
    far_weights, base, far, total = refs
    kk = pl.program_id(1)
    term = nt(hid[...], wide([weights[g] for g in range(group)]))

    @pl.when(kk == 0)
    def _():
        total[...] = term
        far[...] = nt(hid[...], wide([far_weights[g] for g in range(group)])).astype(BF16)

    @pl.when(kk > 0)
    def _():
        total[...] += term

    @pl.when(kk == near - 1)
    def _():
        base[...] = total[...]


def near_call(hidden, first, count_in, near):
    rows = hidden.shape[0]
    _, hid_count, links, size, _ = first.shape
    group = hid_count // count_in

    def mate(c, kk):
        return c ^ ((1 << kk) >> 1)

    width = count_in * size
    return pl.pallas_call(
        functools.partial(near_kernel, near, group),
        grid=(count_in, near),
        in_specs=[
            pl.BlockSpec((rows, group * size), lambda c, kk: (0, mate(c, kk))),
            pl.BlockSpec(
                (None, group, None, size, size), lambda c, kk: (0, mate(c, kk), kk, 0, 0)
            ),
            pl.BlockSpec((None, group, None, size, size), lambda c, kk: (0, c, near, 0, 0)),
        ],
        out_specs=[
            pl.BlockSpec((rows, size), lambda c, kk: (0, c)),
            pl.BlockSpec((rows, size), lambda c, kk: (0, c)),
        ],
        out_shape=[
            jax.ShapeDtypeStruct((rows, width), F32),
            jax.ShapeDtypeStruct((rows, width), BF16),
        ],
        scratch_shapes=[pltpu.VMEM((rows, size), F32)],
        name="near_parts",
        **params(2),
    )(hidden, first, first)


def second_kernel(links, chunks, rows, *refs):
    ups, refs = refs[: links * chunks], refs[links * chunks :]
    proj, act, out, left_two, up_all = refs
    size = act.shape[1]

    @pl.when(pl.program_id(1) == 0)
    def _():
        for m in range(chunks):
            for k in range(links):
                up_all[m * rows : (m + 1) * rows, k * size : (k + 1) * size] = ups[m * links + k][
                    ...
                ]
        up_all[:, links * size :] = proj[...]

    grads = nn(act[...].T, up_all[...]).astype(BF16)
    for k in range(links):
        out[k] = grads[:, k * size : (k + 1) * size]
    left_two[...] = grads[:, links * size :]


def second_call(ups, flips, proj, act, shape):
    chunks = len(ups)
    tokens = act.shape[0]
    rows = tokens // chunks
    _, hid_count, links, size, _ = shape
    count_in = ups[0][0][0].shape[1] // size
    group = hid_count // count_in
    rank = proj.shape[1]
    in_specs = [
        pl.BlockSpec((rows, size), lambda c, j, flip=flip, place=place: (place, c ^ flip))
        for chunk in ups
        for (_, place), flip in zip(chunk, flips)
    ]
    in_specs.append(pl.BlockSpec((tokens, rank), lambda c, j: (0, 0)))
    in_specs.append(pl.BlockSpec((tokens, size), lambda c, j: (0, c * group + j)))
    width = hid_count * size
    return pl.pallas_call(
        functools.partial(second_kernel, links, chunks, rows),
        grid=(count_in, group),
        in_specs=in_specs,
        out_specs=[
            pl.BlockSpec(
                (None, None, links, size, size), lambda c, j: (0, c * group + j, 0, 0, 0)
            ),
            pl.BlockSpec((None, size, rank), lambda c, j: (0, c * group + j, 0)),
        ],
        out_shape=[
            jax.ShapeDtypeStruct(shape, BF16),
            jax.ShapeDtypeStruct((1, width, rank), BF16),
        ],
        scratch_shapes=[pltpu.VMEM((tokens, links * size + rank), BF16)],
        name="second_grad",
        **params(2),
    )(*[up for chunk in ups for up, _ in chunk], proj, act)


def first_kernel(links, chunks, rows, *refs):
    ins, refs = refs[: links * chunks], refs[links * chunks :]
    proj, refs = refs[0], refs[1:]
    hids, refs = refs[:1], refs[1:]
    out, right_one, in_all = refs
    size = hids[0].shape[1]

    @pl.when(pl.program_id(1) == 0)
    def _():
        for m in range(chunks):
            for k in range(links):
                in_all[k * size : (k + 1) * size, m * rows : (m + 1) * rows] = ins[m * links + k][
                    ...
                ].T
        in_all[links * size :, :] = proj[...].T

    hid = jnp.concatenate([ref[...] for ref in hids], axis=0)
    grads = nn(in_all[...], hid).astype(BF16)
    for k in range(links):
        out[k] = grads[k * size : (k + 1) * size]
    right_one[...] = grads[links * size :]


def first_call(ins, flips, proj, hids, shape):
    chunks = len(ins)
    tokens = hids[0].shape[0]
    rows = tokens // chunks
    _, hid_count, links, size, _ = shape
    count_in = ins[0][0][0].shape[1] // size
    group = hid_count // count_in
    rank = proj.shape[1]
    in_specs = [
        pl.BlockSpec((rows, size), lambda c, j, flip=flip, place=place: (place, c ^ flip))
        for chunk in ins
        for (_, place), flip in zip(chunk, flips)
    ]
    in_specs.append(pl.BlockSpec((tokens, rank), lambda c, j: (0, 0)))
    in_specs += [pl.BlockSpec((tokens, size), lambda c, j: (0, c * group + j))]
    width = hid_count * size
    return pl.pallas_call(
        functools.partial(first_kernel, links, chunks, rows),
        grid=(count_in, group),
        in_specs=in_specs,
        out_specs=[
            pl.BlockSpec(
                (None, None, links, size, size), lambda c, j: (0, c * group + j, 0, 0, 0)
            ),
            pl.BlockSpec((None, rank, size), lambda c, j: (0, 0, c * group + j)),
        ],
        out_shape=[
            jax.ShapeDtypeStruct(shape, BF16),
            jax.ShapeDtypeStruct((1, rank, width), BF16),
        ],
        scratch_shapes=[pltpu.VMEM((links * size + rank, tokens), BF16)],
        name="first_grad",
        **params(2),
    )(*[value for chunk in ins for value, _ in chunk], proj, *hids)


def body(
    inputs, preact, handoff, first_blocks, second_blocks, left_one, right_one, left_two, right_two
):
    shape = first_blocks.shape
    links, size = shape[2], shape[-1]
    tokens, feats = inputs.shape[1:]
    count_in = feats // size
    near = count_in.bit_length()
    flips = [(1 << k) >> 1 if k < near else 0 for k in range(links)]
    rows = tokens // CHUNKS
    spans = [slice(m * rows, (m + 1) * rows) for m in range(CHUNKS)]

    def sent(value):
        far = [swapped(value, bit) for bit in reversed(range(1, links - near))]
        return far[::-1]

    ranks = left_one.shape[2]
    first_half, second_half = spans

    in_core = swapped(inputs[0], 0)
    in_one = sent(inputs[0, first_half])
    act, slope, proj_act = gate_call(preact, left_two, size)
    early = jnp.concatenate([nn(inputs[0], left_one[0]), proj_act], axis=1)

    upstream = after(shifted(handoff[0]), in_core, early, *in_one)
    up_far = sent(upstream)
    up_core = swapped(upstream, 0)
    sums = tree_sum(jnp.concatenate([nt(upstream, right_two[0]), early], axis=1))
    proj_grad, proj_in, proj_act = jnp.split(sums, (ranks, 2 * ranks), axis=1)
    up_set = [(value, 0) for value in [upstream] * near + [up_core] + up_far]

    in_two = sent(after(inputs[0, second_half], sums, *up_far))
    hidden, *parts, back = hidden_call(
        up_set,
        flips,
        proj_grad,
        second_blocks,
        left_two,
        slope,
        right_one,
        first_blocks,
        near + 1,
        0,
    )

    def returned(pieces):
        return [swapped(piece, k + 1) for k, piece in reversed(list(enumerate(pieces)))]

    far_one, far_two = [returned(parts[m::CHUNKS]) for m in range(CHUNKS)]
    second_grad, lefttwo_grad = second_call([up_set], flips, after(proj_grad, back), act, shape)
    base, beside = near_call(after(hidden, second_grad), first_blocks, count_in, near)
    beside = swapped(beside, 0)
    back_rank = tree_sum(after(back, base, *in_two, *far_one))
    in_sets = [
        [(inputs[0], m)] * near + [(in_core, m)] + [(value, 0) for value in values]
        for m, values in enumerate([in_one, in_two])
    ]
    first_grad, rightone_grad = first_call(
        in_sets, flips, after(proj_in, beside), [hidden], shape
    )
    base = base + beside.astype(F32) + nt(back_rank, left_one[0])
    leftone_grad = nn(inputs[0].T, back_rank).astype(BF16)[None]
    righttwo_grad = nn(proj_act.T, upstream).astype(BF16)[None]
    total, first_grad, leftone_grad, righttwo_grad = lax.optimization_barrier(
        (base, first_grad, leftone_grad, righttwo_grad)
    )
    for pair in zip(far_one, far_two):
        total = total + jnp.concatenate(pair, axis=0).astype(F32)
    input_grad = total.astype(BF16)[None]
    return (
        input_grad,
        first_grad,
        second_grad,
        leftone_grad,
        rightone_grad,
        lefttwo_grad,
        righttwo_grad,
    )


def solution(mesh):
    by_feature = P("section", None, "tensor")
    by_block = P("section", "tensor", None, None, None)
    by_row = P("section", "tensor", None)
    in_specs = (
        by_feature,
        by_feature,
        by_feature,
        by_block,
        by_block,
        by_row,
        by_feature,
        by_row,
        by_feature,
    )
    out_specs = (
        by_feature,
        by_block,
        by_block,
        by_row,
        by_feature,
        by_row,
        by_feature,
    )
    return jax.shard_map(body, mesh=mesh, in_specs=in_specs, out_specs=out_specs, check_vma=False)
```

```python
import functools

import jax
import jax.numpy as jnp
from jax import lax
from jax.experimental import pallas as pl
from jax.experimental.pallas import tpu as pltpu
from jax.sharding import PartitionSpec as P

CHUNKS = 2
BF16 = jnp.bfloat16
F32 = jnp.float32


def swapped(value, bit):
    pairs = [(source, source ^ (1 << bit)) for source in range(lax.axis_size("tensor"))]
    return lax.ppermute(value, "tensor", pairs)


def shifted(value):
    peers = lax.axis_size("section")
    return lax.ppermute(value, "section", [(i, (i - 1) % peers) for i in range(peers)])


def tree_sum(value, halvings, before_swap=(), before_gather=()):
    bits = lax.axis_size("tensor").bit_length() - 1
    place = lax.axis_index("tensor")
    for bit in range(halvings):
        half = value.shape[0] // 2
        mine = (place >> bit) & 1
        keep = lax.dynamic_slice_in_dim(value, mine * half, half)
        give = lax.dynamic_slice_in_dim(value, (1 - mine) * half, half)
        give = give if bit == 0 else give.astype(BF16)
        value = keep + swapped(give, bit).astype(F32)
    value = after(value, *before_swap)
    stages = []
    for bit in range(halvings, bits):
        value = value + swapped(value.astype(BF16), bit).astype(F32)
        stages.append(value)
    value = after(value.astype(BF16), *before_gather)
    for bit in reversed(range(halvings)):
        mine = (place >> bit) & 1
        other = swapped(value, bit)
        first = jnp.where(mine == 0, value, other)
        second = jnp.where(mine == 0, other, value)
        value = jnp.concatenate([first, second])
    return value, stages[0]


def nt(left, right):
    return lax.dot_general(left, right, (((1,), (1,)), ((), ())), preferred_element_type=F32)


def nn(left, right):
    return jnp.dot(left, right, preferred_element_type=F32)


def wide(parts):
    return parts[0] if len(parts) == 1 else jnp.concatenate(parts, axis=1)


def after(value, *others):
    return lax.optimization_barrier((value, *others))[0]


def gate_kernel(strip, preact, left_two, act, slope, proj):
    def one(r, _):
        rows = pl.ds(pl.multiple_of(r * strip, strip), strip)
        values = preact[rows, :].astype(F32)
        normal_cdf = 0.5 * (1.0 + lax.erf(values * 0.7071067811865476))
        density = jnp.exp(-0.5 * values * values) * 0.3989422804014327
        act[rows, :] = (values * normal_cdf).astype(BF16)
        slope[rows, :] = normal_cdf + values * density
        return 0

    lax.fori_loop(0, preact.shape[0] // strip, one, 0)
    term = nn(act[...], left_two[...])

    @pl.when(pl.program_id(0) == 0)
    def _():
        proj[...] = term

    @pl.when(pl.program_id(0) > 0)
    def _():
        proj[...] += term


def gate_call(preact, left_two, size):
    _, tokens, width = preact.shape
    rank = left_two.shape[2]
    return pl.pallas_call(
        functools.partial(gate_kernel, min(64, tokens)),
        grid=(width // size,),
        in_specs=[
            pl.BlockSpec((None, tokens, size), lambda i: (0, 0, i)),
            pl.BlockSpec((None, size, rank), lambda i: (0, i, 0)),
        ],
        out_specs=[
            pl.BlockSpec((tokens, size), lambda i: (0, i)),
            pl.BlockSpec((tokens, size), lambda i: (0, i)),
            pl.BlockSpec((tokens, rank), lambda i: (0, 0)),
        ],
        out_shape=[
            jax.ShapeDtypeStruct((tokens, width), BF16),
            jax.ShapeDtypeStruct((tokens, width), F32),
            jax.ShapeDtypeStruct((tokens, rank), F32),
        ],
        name="gate",
        **params(1),
    )(preact, left_two)


def params(steps):
    return dict(
        cost_estimate=pl.CostEstimate(flops=1024, bytes_accessed=1024, transcendentals=0),
        compiler_params=pltpu.CompilerParams(
            dimension_semantics=("arbitrary",) * steps, vmem_limit_bytes=56 * 2**20
        ),
    )


def hidden_kernel(links, late, group, *refs):
    ups, refs = refs[:links], refs[links:]
    proj, refs = refs[0], refs[1:]
    seconds, refs = refs[:links], refs[links:]
    left_two, slope, right_one, refs = refs[0], refs[1], refs[2], refs[3:]
    firsts, refs = refs[:late], refs[late:]
    hidden, refs = refs[0], refs[1:]
    parts, refs = refs[: late * CHUNKS], refs[late * CHUNKS :]
    rank, up_all, hid_all = refs
    c, j = pl.program_id(0), pl.program_id(1)
    size = hidden.shape[1]

    @pl.when(j == 0)
    def _():
        for k in range(links):
            up_all[:, k * size : (k + 1) * size] = ups[k][...]
        up_all[:, links * size :] = proj[...]

    weights = wide([ref[...] for ref in seconds] + [left_two[...]])
    grad = nt(up_all[...], weights)
    hid = (grad * slope[...]).astype(BF16)
    hidden[...] = hid
    hid_all[:, pl.ds(pl.multiple_of(j * size, size), size)] = hid

    @pl.when(j == group - 1)
    def _():
        group_grad = hid_all[...]
        for n, ref in enumerate(firsts):
            part = nt(group_grad, wide([ref[g] for g in range(group)])).astype(BF16)
            for m in range(CHUNKS):
                piece = parts[n * CHUNKS + m]
                piece[...] = part[m * piece.shape[0] : (m + 1) * piece.shape[0]]
        term = nt(group_grad, right_one[...])

        @pl.when(c == 0)
        def _():
            rank[...] = term

        @pl.when(c > 0)
        def _():
            rank[...] += term


def hidden_call(ups, flips, proj, second, left_two, slope, right_one, first, late_from, chunk):
    rows = ups[-1][0].shape[0]
    _, hid_count, links, size, _ = first.shape
    count_in = ups[0][0].shape[1] // size
    group = hid_count // count_in
    rank = proj.shape[1]
    late = links - late_from
    in_specs = [
        pl.BlockSpec((rows, size), lambda c, j, flip=flip, place=place: (place, c ^ flip))
        for (_, place), flip in zip(ups, flips)
    ]
    in_specs.append(pl.BlockSpec((rows, rank), lambda c, j: (chunk, 0)))
    in_specs += [
        pl.BlockSpec((None, None, None, size, size), lambda c, j, k=k: (0, c * group + j, k, 0, 0))
        for k in range(links)
    ]
    in_specs.append(pl.BlockSpec((None, size, rank), lambda c, j: (0, c * group + j, 0)))
    in_specs.append(pl.BlockSpec((rows, size), lambda c, j: (chunk, c * group + j)))
    in_specs.append(pl.BlockSpec((None, rank, group * size), lambda c, j: (0, 0, c)))
    in_specs += [
        pl.BlockSpec((None, group, None, size, size), lambda c, j, k=k: (0, c, k, 0, 0))
        for k in range(late_from, links)
    ]
    out_specs = [pl.BlockSpec((rows, size), lambda c, j: (0, c * group + j))]
    out_specs += [pl.BlockSpec((rows // CHUNKS, size), lambda c, j: (0, c))] * (late * CHUNKS)
    out_specs.append(pl.BlockSpec((rows, rank), lambda c, j: (0, 0)))
    width = hid_count * size
    out_shape = [jax.ShapeDtypeStruct((rows, width), BF16)]
    out_shape += [
        jax.ShapeDtypeStruct((rows // CHUNKS, count_in * size), BF16)
    ] * (late * CHUNKS)
    out_shape.append(jax.ShapeDtypeStruct((rows, rank), F32))
    return pl.pallas_call(
        functools.partial(hidden_kernel, links, late, group),
        grid=(count_in, group),
        in_specs=in_specs,
        out_specs=out_specs,
        out_shape=out_shape,
        scratch_shapes=[
            pltpu.VMEM((rows, links * size + rank), BF16),
            pltpu.VMEM((rows, group * size), BF16),
        ],
        name="hidden_grad",
        **params(2),
    )(
        *[up for up, _ in ups], proj, *[second] * links, left_two, slope, right_one, *[first] * late
    )


def near_kernel(near, group, hid, *refs):
    weights, refs = refs[0], refs[1:]
    far_weights, base, *far, total = refs
    kk = pl.program_id(1)
    term = nt(hid[...], wide([weights[g] for g in range(group)]))

    @pl.when(kk == 0)
    def _():
        total[...] = term
        other = nt(hid[...], wide([far_weights[g] for g in range(group)])).astype(BF16)
        for m, piece in enumerate(far):
            piece[...] = other[m * piece.shape[0] : (m + 1) * piece.shape[0]]

    @pl.when(kk > 0)
    def _():
        total[...] += term

    @pl.when(kk == near - 1)
    def _():
        base[...] = total[...]


def near_call(hidden, first, count_in, near):
    rows = hidden.shape[0]
    _, hid_count, links, size, _ = first.shape
    group = hid_count // count_in

    def mate(c, kk):
        return c ^ ((1 << kk) >> 1)

    width = count_in * size
    return pl.pallas_call(
        functools.partial(near_kernel, near, group),
        grid=(count_in, near),
        in_specs=[
            pl.BlockSpec((rows, group * size), lambda c, kk: (0, mate(c, kk))),
            pl.BlockSpec(
                (None, group, None, size, size), lambda c, kk: (0, mate(c, kk), kk, 0, 0)
            ),
            pl.BlockSpec((None, group, None, size, size), lambda c, kk: (0, c, near, 0, 0)),
        ],
        out_specs=[
            pl.BlockSpec((rows, size), lambda c, kk: (0, c)),
            *[pl.BlockSpec((rows // CHUNKS, size), lambda c, kk: (0, c))] * CHUNKS,
        ],
        out_shape=[
            jax.ShapeDtypeStruct((rows, width), F32),
            *[jax.ShapeDtypeStruct((rows // CHUNKS, width), BF16)] * CHUNKS,
        ],
        scratch_shapes=[pltpu.VMEM((rows, size), F32)],
        name="near_parts",
        **params(2),
    )(hidden, first, first)


def second_kernel(count, group, has_proj, *refs):
    ups, refs = refs[:count], refs[count:]
    if has_proj:
        proj, act, _, out, left_two, turned = refs
    else:
        act, out, turned = refs
    k = pl.program_id(1)
    size = ups[0].shape[1]

    @pl.when(k == 0)
    def _():
        for g in range(group):
            turned[g * size : (g + 1) * size, :] = act[:, g * size : (g + 1) * size].T

    def store(up):
        grads = nn(turned[...], up).astype(BF16)
        for g in range(group):
            out[g] = grads[g * size : (g + 1) * size]

    for n in range(count):
        pl.when(k == n)(lambda n=n: store(ups[n][...]))

    if has_proj:

        @pl.when(k == count - 1)
        def _():
            left_two[...] = nn(turned[...], proj[...]).astype(BF16)


def second_call(ups, flips, act, shape, start, proj=None, partial=None):
    count = len(ups)
    tokens = act.shape[0]
    _, hid_count, links, size, _ = shape
    count_in = ups[0].shape[1] // size
    group = hid_count // count_in
    has_proj = proj is not None
    in_specs = [
        pl.BlockSpec((tokens, size), lambda c, k, flip=flip: (0, c ^ flip)) for flip in flips
    ]
    args = list(ups)
    out_specs = [
        pl.BlockSpec((None, group, None, size, size), lambda c, k: (0, c, start + k, 0, 0))
    ]
    out_shape = [jax.ShapeDtypeStruct(shape, BF16)]
    aliases = {}
    if has_proj:
        rank = proj.shape[1]
        in_specs.append(pl.BlockSpec((tokens, rank), lambda c, k: (0, 0)))
        args.append(proj)
        out_specs.append(pl.BlockSpec((None, group * size, rank), lambda c, k: (0, c, 0)))
        out_shape.append(jax.ShapeDtypeStruct((1, hid_count * size, rank), BF16))
    in_specs.append(pl.BlockSpec((tokens, group * size), lambda c, k: (0, c)))
    args.append(act)
    if has_proj:
        in_specs.append(pl.BlockSpec(memory_space=pl.ANY))
        args.append(partial)
        aliases = {len(args) - 1: 0}
    return pl.pallas_call(
        functools.partial(second_kernel, count, group, has_proj),
        grid=(count_in, count),
        in_specs=in_specs,
        out_specs=out_specs,
        out_shape=out_shape,
        scratch_shapes=[pltpu.VMEM((group * size, tokens), BF16)],
        input_output_aliases=aliases,
        name="second_late" if has_proj else "second_early",
        **params(2),
    )(*args)


def first_kernel(links, chunks, rows, *refs):
    ins, refs = refs[: links * chunks], refs[links * chunks :]
    proj, refs = refs[0], refs[1:]
    hids, refs = refs[:1], refs[1:]
    out, right_one, in_all = refs
    size = hids[0].shape[1]

    @pl.when(pl.program_id(1) == 0)
    def _():
        for m in range(chunks):
            for k in range(links):
                in_all[k * size : (k + 1) * size, m * rows : (m + 1) * rows] = ins[m * links + k][
                    ...
                ].T
        in_all[links * size :, :] = proj[...].T

    hid = jnp.concatenate([ref[...] for ref in hids], axis=0)
    grads = nn(in_all[...], hid).astype(BF16)
    for k in range(links):
        out[k] = grads[k * size : (k + 1) * size]
    right_one[...] = grads[links * size :]


def first_call(ins, flips, proj, hids, shape):
    chunks = len(ins)
    tokens = hids[0].shape[0]
    rows = tokens // chunks
    _, hid_count, links, size, _ = shape
    count_in = ins[0][0][0].shape[1] // size
    group = hid_count // count_in
    rank = proj.shape[1]
    in_specs = [
        pl.BlockSpec((rows, size), lambda c, j, flip=flip, place=place: (place, c ^ flip))
        for chunk in ins
        for (_, place), flip in zip(chunk, flips)
    ]
    in_specs.append(pl.BlockSpec((tokens, rank), lambda c, j: (0, 0)))
    in_specs += [pl.BlockSpec((tokens, size), lambda c, j: (0, c * group + j))]
    width = hid_count * size
    return pl.pallas_call(
        functools.partial(first_kernel, links, chunks, rows),
        grid=(count_in, group),
        in_specs=in_specs,
        out_specs=[
            pl.BlockSpec(
                (None, None, links, size, size), lambda c, j: (0, c * group + j, 0, 0, 0)
            ),
            pl.BlockSpec((None, rank, size), lambda c, j: (0, 0, c * group + j)),
        ],
        out_shape=[
            jax.ShapeDtypeStruct(shape, BF16),
            jax.ShapeDtypeStruct((1, rank, width), BF16),
        ],
        scratch_shapes=[pltpu.VMEM((links * size + rank, tokens), BF16)],
        name="first_grad",
        **params(2),
    )(*[value for chunk in ins for value, _ in chunk], proj, *hids)


def body(
    inputs, preact, handoff, first_blocks, second_blocks, left_one, right_one, left_two, right_two
):
    shape = first_blocks.shape
    links, size = shape[2], shape[-1]
    tokens, feats = inputs.shape[1:]
    count_in = feats // size
    near = count_in.bit_length()
    flips = [(1 << k) >> 1 if k < near else 0 for k in range(links)]
    rows = tokens // CHUNKS
    spans = [slice(m * rows, (m + 1) * rows) for m in range(CHUNKS)]

    def sent(value):
        far = [swapped(value, bit) for bit in reversed(range(1, links - near))]
        return far[::-1]

    ranks = left_one.shape[2]
    first_half, second_half = spans

    in_core = swapped(inputs[0], 0)
    in_one = sent(inputs[0, first_half])
    act, slope, proj_act = gate_call(preact, left_two, size)
    early = jnp.concatenate([nn(inputs[0], left_one[0]), proj_act], axis=1)

    upstream = after(shifted(handoff[0]), in_core, early, *in_one)
    up_far = sent(upstream)
    up_core = swapped(upstream, 0)
    (second_part,) = second_call(
        [upstream] * near + [up_core], flips[: near + 1], act, shape, 0
    )
    sums, _ = tree_sum(
        jnp.concatenate([nt(upstream, right_two[0]), early], axis=1),
        links - near - 1,
        [second_part],
        up_far,
    )
    proj_grad, proj_in, proj_act = jnp.split(sums, (ranks, 2 * ranks), axis=1)
    up_set = [(value, 0) for value in [upstream] * near + [up_core] + up_far]

    in_two = sent(after(inputs[0], *up_far)[second_half])
    hidden, *parts, back = hidden_call(
        up_set,
        flips,
        proj_grad,
        second_blocks,
        left_two,
        slope,
        right_one,
        first_blocks,
        near + 1,
        0,
    )

    def returned(pieces):
        return [swapped(piece, k + 1) for k, piece in reversed(list(enumerate(pieces)))]

    back, *parts = lax.optimization_barrier((back, *parts, *in_two))[: 1 + len(parts)]
    far_one = returned(parts[::CHUNKS])
    parts = parts[1::CHUNKS]
    far_two = returned(lax.optimization_barrier((*parts, *far_one))[: len(parts)])
    back_rank, stage = tree_sum(back, 1)
    base, *beside = near_call(hidden, first_blocks, count_in, near)
    beside = jnp.concatenate([swapped(piece, 0) for piece in beside], axis=0)
    second_grad, lefttwo_grad = second_call(
        up_far, flips[near + 1 :], act, shape, near + 1, after(proj_grad, stage), second_part
    )
    in_sets = [
        [(inputs[0], m)] * near + [(in_core, m)] + [(value, 0) for value in values]
        for m, values in enumerate([in_one, in_two])
    ]
    first_grad, rightone_grad = first_call(
        in_sets, flips, after(proj_in, *far_one), [hidden], shape
    )
    base = base + beside.astype(F32) + nt(back_rank, left_one[0])
    leftone_grad = nn(inputs[0].T, back_rank).astype(BF16)[None]
    righttwo_grad = nn(proj_act.T, upstream).astype(BF16)[None]
    total, first_grad, leftone_grad, righttwo_grad = lax.optimization_barrier(
        (base, first_grad, leftone_grad, righttwo_grad)
    )
    for pair in zip(far_one, far_two):
        total = total + jnp.concatenate(pair, axis=0).astype(F32)
    input_grad = total.astype(BF16)[None]
    return (
        input_grad,
        first_grad,
        second_grad,
        leftone_grad,
        rightone_grad,
        lefttwo_grad,
        righttwo_grad,
    )


def solution(mesh):
    by_feature = P("section", None, "tensor")
    by_block = P("section", "tensor", None, None, None)
    by_row = P("section", "tensor", None)
    in_specs = (
        by_feature,
        by_feature,
        by_feature,
        by_block,
        by_block,
        by_row,
        by_feature,
        by_row,
        by_feature,
    )
    out_specs = (
        by_feature,
        by_block,
        by_block,
        by_row,
        by_feature,
        by_row,
        by_feature,
    )
    return jax.shard_map(body, mesh=mesh, in_specs=in_specs, out_specs=out_specs, check_vma=False)
```

```python
import functools

import jax
import jax.numpy as jnp
from jax import lax
from jax.experimental import pallas as pl
from jax.experimental.pallas import tpu as pltpu
from jax.sharding import PartitionSpec as P

UP_SHARES = ((3, 0, 5), (4, 4, 0))
BACK_SHARES = ((2, 4, 2), (7, 1, 0))
BF16 = jnp.bfloat16
F32 = jnp.float32


def swapped(value, bit):
    pairs = [(source, source ^ (1 << bit)) for source in range(lax.axis_size("tensor"))]
    return lax.ppermute(value, "tensor", pairs)


def shifted(value):
    peers = lax.axis_size("section")
    return lax.ppermute(value, "section", [(i, (i - 1) % peers) for i in range(peers)])


def halved(value, bit, work=()):
    half = value.shape[0] // 2
    mine = (lax.axis_index("tensor") >> bit) & 1
    keep = lax.dynamic_slice_in_dim(value, mine * half, half)
    give = lax.dynamic_slice_in_dim(value, (1 - mine) * half, half)
    give = give if bit == 0 else give.astype(BF16)
    return keep + after(swapped(give, bit), *work).astype(F32)


def gathered(value, bit):
    mine = (lax.axis_index("tensor") >> bit) & 1
    other = swapped(value, bit)
    first = jnp.where(mine == 0, value, other)
    second = jnp.where(mine == 0, other, value)
    return jnp.concatenate([first, second])


def shares_of(shares, count):
    return [shares[0]] * (count - 1) + [shares[1]]


def cut(value, shares):
    pieces, start = [], 0
    for share in shares:
        stop = start + value.shape[0] * share // 8
        pieces.append(value[start:stop] if share else None)
        start = stop
    return pieces


def sent(piece, bit, *others):
    return None if piece is None else swapped(after(piece, *others), bit)


def kept(pieces):
    return [piece for piece in pieces if piece is not None]


def relay(links, value, work):
    last = len(links)
    firsts = [sent(link[0], bit) for bit, link in enumerate(links, 1)]
    value = halved(value, 0)
    done = work(value)
    seconds = [sent(link[1], bit, value) for bit, link in enumerate(links[:-1], 1)]
    for bit in range(1, last):
        value = halved(value, bit, done if bit == 1 else ())
    value = after(value, *firsts)
    seconds.append(sent(links[-1][1], last, value))
    value = (value + swapped(value.astype(BF16), last).astype(F32)).astype(BF16)
    thirds = [sent(link[2], bit, value) for bit, link in enumerate(links, 1)]
    value = after(value, *kept(seconds[:-1]))
    for bit in reversed(range(1, last)):
        value = gathered(value, bit)
    value = gathered(after(value, seconds[-1]), 0)
    return value, [kept(link) for link in zip(firsts, seconds, thirds)]


def nt(left, right):
    return lax.dot_general(left, right, (((1,), (1,)), ((), ())), preferred_element_type=F32)


def nn(left, right):
    return jnp.dot(left, right, preferred_element_type=F32)


def wide(parts):
    return parts[0] if len(parts) == 1 else jnp.concatenate(parts, axis=1)


def after(value, *others):
    return lax.optimization_barrier((value, *others))[0]


def gate_kernel(strip, preact, left_two, act, slope, proj):
    def one(r, _):
        rows = pl.ds(pl.multiple_of(r * strip, strip), strip)
        values = preact[rows, :].astype(F32)
        normal_cdf = 0.5 * (1.0 + lax.erf(values * 0.7071067811865476))
        density = jnp.exp(-0.5 * values * values) * 0.3989422804014327
        act[rows, :] = (values * normal_cdf).astype(BF16)
        slope[rows, :] = normal_cdf + values * density
        return 0

    lax.fori_loop(0, preact.shape[0] // strip, one, 0)
    term = nn(act[...], left_two[...])

    @pl.when(pl.program_id(0) == 0)
    def _():
        proj[...] = term

    @pl.when(pl.program_id(0) > 0)
    def _():
        proj[...] += term


def gate_call(preact, left_two, size):
    _, tokens, width = preact.shape
    rank = left_two.shape[2]
    return pl.pallas_call(
        functools.partial(gate_kernel, min(64, tokens)),
        grid=(width // size,),
        in_specs=[
            pl.BlockSpec((None, tokens, size), lambda i: (0, 0, i)),
            pl.BlockSpec((None, size, rank), lambda i: (0, i, 0)),
        ],
        out_specs=[
            pl.BlockSpec((tokens, size), lambda i: (0, i)),
            pl.BlockSpec((tokens, size), lambda i: (0, i)),
            pl.BlockSpec((tokens, rank), lambda i: (0, 0)),
        ],
        out_shape=[
            jax.ShapeDtypeStruct((tokens, width), BF16),
            jax.ShapeDtypeStruct((tokens, width), F32),
            jax.ShapeDtypeStruct((tokens, rank), F32),
        ],
        name="gate",
        **params(1),
    )(preact, left_two)


def params(steps):
    return dict(
        cost_estimate=pl.CostEstimate(flops=1024, bytes_accessed=1024, transcendentals=0),
        compiler_params=pltpu.CompilerParams(
            dimension_semantics=("arbitrary",) * steps, vmem_limit_bytes=56 * 2**20
        ),
    )


def taken(refs, counts):
    groups = []
    for count in counts:
        groups.append(refs[:count])
        refs = refs[count:]
    return groups, refs


def hidden_kernel(counts, part_counts, group, *refs):
    links, late = len(counts), len(part_counts)
    ups, refs = taken(refs, counts)
    proj, refs = refs[0], refs[1:]
    seconds, refs = refs[:links], refs[links:]
    left_two, slope, right_one, refs = refs[0], refs[1], refs[2], refs[3:]
    firsts, refs = refs[:late], refs[late:]
    hidden, refs = refs[0], refs[1:]
    parts, refs = taken(refs, part_counts)
    rank, up_all, hid_all = refs
    c, j = pl.program_id(0), pl.program_id(1)
    size = hidden.shape[1]

    @pl.when(j == 0)
    def _():
        for k in range(links):
            start = 0
            for piece in ups[k]:
                stop = start + piece.shape[0]
                up_all[start:stop, k * size : (k + 1) * size] = piece[...]
                start = stop
        up_all[:, links * size :] = proj[...]

    weights = wide([ref[...] for ref in seconds] + [left_two[...]])
    grad = nt(up_all[...], weights)
    hid = (grad * slope[...]).astype(BF16)
    hidden[...] = hid
    hid_all[:, pl.ds(pl.multiple_of(j * size, size), size)] = hid

    @pl.when(j == group - 1)
    def _():
        group_grad = hid_all[...]
        for n, ref in enumerate(firsts):
            part = nt(group_grad, wide([ref[g] for g in range(group)])).astype(BF16)
            start = 0
            for piece in parts[n]:
                stop = start + piece.shape[0]
                piece[...] = part[start:stop]
                start = stop
        term = nt(group_grad, right_one[...])

        @pl.when(c == 0)
        def _():
            rank[...] = term

        @pl.when(c > 0)
        def _():
            rank[...] += term


def piece_specs(sets, flips, size):
    return [
        pl.BlockSpec((piece.shape[0], size), lambda c, j, flip=flip: (0, c ^ flip))
        for pieces, flip in zip(sets, flips)
        for piece in pieces
    ]


def hidden_call(ups, flips, proj, second, left_two, slope, right_one, first, late_from):
    rows, width = slope.shape
    _, hid_count, links, size, _ = first.shape
    count_in = ups[0][0].shape[1] // size
    group = hid_count // count_in
    rank = proj.shape[1]
    late = links - late_from
    shares = [[rows * n // 8 for n in link if n] for link in shares_of(BACK_SHARES, late)]
    pieces = [n for link in shares for n in link]
    in_specs = piece_specs(ups, flips, size)
    in_specs.append(pl.BlockSpec((rows, rank), lambda c, j: (0, 0)))
    in_specs += [
        pl.BlockSpec((None, None, None, size, size), lambda c, j, k=k: (0, c * group + j, k, 0, 0))
        for k in range(links)
    ]
    in_specs.append(pl.BlockSpec((None, size, rank), lambda c, j: (0, c * group + j, 0)))
    in_specs.append(pl.BlockSpec((rows, size), lambda c, j: (0, c * group + j)))
    in_specs.append(pl.BlockSpec((None, rank, group * size), lambda c, j: (0, 0, c)))
    in_specs += [
        pl.BlockSpec((None, group, None, size, size), lambda c, j, k=k: (0, c, k, 0, 0))
        for k in range(late_from, links)
    ]
    out_specs = [pl.BlockSpec((rows, size), lambda c, j: (0, c * group + j))]
    out_specs += [pl.BlockSpec((n, size), lambda c, j: (0, c)) for n in pieces]
    out_specs.append(pl.BlockSpec((rows, rank), lambda c, j: (0, 0)))
    out_shape = [jax.ShapeDtypeStruct((rows, width), BF16)]
    out_shape += [jax.ShapeDtypeStruct((n, count_in * size), BF16) for n in pieces]
    out_shape.append(jax.ShapeDtypeStruct((rows, rank), F32))
    return pl.pallas_call(
        functools.partial(
            hidden_kernel, [len(link) for link in ups], [len(link) for link in shares], group
        ),
        grid=(count_in, group),
        in_specs=in_specs,
        out_specs=out_specs,
        out_shape=out_shape,
        scratch_shapes=[
            pltpu.VMEM((rows, links * size + rank), BF16),
            pltpu.VMEM((rows, group * size), BF16),
        ],
        name="hidden_grad",
        **params(2),
    )(
        *[piece for link in ups for piece in link], proj, *[second] * links, left_two, slope, right_one, *[first] * late
    )


def near_kernel(near, group, hid, *refs):
    weights, refs = refs[0], refs[1:]
    far_weights, base, *far, total = refs
    kk = pl.program_id(1)
    term = nt(hid[...], wide([weights[g] for g in range(group)]))

    @pl.when(kk == 0)
    def _():
        total[...] = term
        other = nt(hid[...], wide([far_weights[g] for g in range(group)])).astype(BF16)
        for m, piece in enumerate(far):
            piece[...] = other[m * piece.shape[0] : (m + 1) * piece.shape[0]]

    @pl.when(kk > 0)
    def _():
        total[...] += term

    @pl.when(kk == near - 1)
    def _():
        base[...] = total[...]


def near_call(hidden, first, count_in, near):
    rows = hidden.shape[0]
    _, hid_count, links, size, _ = first.shape
    group = hid_count // count_in

    def mate(c, kk):
        return c ^ ((1 << kk) >> 1)

    width = count_in * size
    return pl.pallas_call(
        functools.partial(near_kernel, near, group),
        grid=(count_in, near),
        in_specs=[
            pl.BlockSpec((rows, group * size), lambda c, kk: (0, mate(c, kk))),
            pl.BlockSpec(
                (None, group, None, size, size), lambda c, kk: (0, mate(c, kk), kk, 0, 0)
            ),
            pl.BlockSpec((None, group, None, size, size), lambda c, kk: (0, c, near, 0, 0)),
        ],
        out_specs=[
            pl.BlockSpec((rows, size), lambda c, kk: (0, c)),
            *[pl.BlockSpec((rows // 2, size), lambda c, kk: (0, c))] * 2,
        ],
        out_shape=[
            jax.ShapeDtypeStruct((rows, width), F32),
            *[jax.ShapeDtypeStruct((rows // 2, width), BF16)] * 2,
        ],
        scratch_shapes=[pltpu.VMEM((rows, size), F32)],
        name="near_parts",
        **params(2),
    )(hidden, first, first)


def second_kernel(counts, group, has_proj, *refs):
    count = len(counts)
    ups, refs = taken(refs, counts)
    if has_proj:
        proj, act, _, out, left_two, turned = refs
    else:
        act, out, turned = refs
    k = pl.program_id(1)
    size = ups[0][0].shape[1]

    @pl.when(k == 0)
    def _():
        for g in range(group):
            turned[g * size : (g + 1) * size, :] = act[:, g * size : (g + 1) * size].T

    def store(pieces):
        up = jnp.concatenate([piece[...] for piece in pieces], axis=0)
        grads = nn(turned[...], up).astype(BF16)
        for g in range(group):
            out[g] = grads[g * size : (g + 1) * size]

    for n in range(count):
        pl.when(k == n)(lambda n=n: store(ups[n]))

    if has_proj:

        @pl.when(k == count - 1)
        def _():
            left_two[...] = nn(turned[...], proj[...]).astype(BF16)


def second_call(ups, flips, act, shape, start, proj=None, partial=None):
    count = len(ups)
    tokens = act.shape[0]
    _, hid_count, links, size, _ = shape
    count_in = ups[0][0].shape[1] // size
    group = hid_count // count_in
    has_proj = proj is not None
    in_specs = piece_specs(ups, flips, size)
    args = [piece for link in ups for piece in link]
    out_specs = [
        pl.BlockSpec((None, group, None, size, size), lambda c, k: (0, c, start + k, 0, 0))
    ]
    out_shape = [jax.ShapeDtypeStruct(shape, BF16)]
    aliases = {}
    if has_proj:
        rank = proj.shape[1]
        in_specs.append(pl.BlockSpec((tokens, rank), lambda c, k: (0, 0)))
        args.append(proj)
        out_specs.append(pl.BlockSpec((None, group * size, rank), lambda c, k: (0, c, 0)))
        out_shape.append(jax.ShapeDtypeStruct((1, hid_count * size, rank), BF16))
    in_specs.append(pl.BlockSpec((tokens, group * size), lambda c, k: (0, c)))
    args.append(act)
    if has_proj:
        in_specs.append(pl.BlockSpec(memory_space=pl.ANY))
        args.append(partial)
        aliases = {len(args) - 1: 0}
    return pl.pallas_call(
        functools.partial(second_kernel, [len(link) for link in ups], group, has_proj),
        grid=(count_in, count),
        in_specs=in_specs,
        out_specs=out_specs,
        out_shape=out_shape,
        scratch_shapes=[pltpu.VMEM((group * size, tokens), BF16)],
        input_output_aliases=aliases,
        name="second_late" if has_proj else "second_early",
        **params(2),
    )(*args)


def first_kernel(counts, *refs):
    links = len(counts)
    ins, refs = taken(refs, counts)
    proj, hid, out, right_one, in_all = refs
    size = hid.shape[1]

    @pl.when(pl.program_id(1) == 0)
    def _():
        for k in range(links):
            start = 0
            for piece in ins[k]:
                stop = start + piece.shape[0]
                in_all[k * size : (k + 1) * size, start:stop] = piece[...].T
                start = stop
        in_all[links * size :, :] = proj[...].T

    grads = nn(in_all[...], hid[...]).astype(BF16)
    for k in range(links):
        out[k] = grads[k * size : (k + 1) * size]
    right_one[...] = grads[links * size :]


def first_call(ins, flips, proj, hidden, shape):
    tokens, width = hidden.shape
    _, hid_count, links, size, _ = shape
    count_in = ins[0][0].shape[1] // size
    group = hid_count // count_in
    rank = proj.shape[1]
    in_specs = piece_specs(ins, flips, size)
    in_specs.append(pl.BlockSpec((tokens, rank), lambda c, j: (0, 0)))
    in_specs.append(pl.BlockSpec((tokens, size), lambda c, j: (0, c * group + j)))
    return pl.pallas_call(
        functools.partial(first_kernel, [len(link) for link in ins]),
        grid=(count_in, group),
        in_specs=in_specs,
        out_specs=[
            pl.BlockSpec(
                (None, None, links, size, size), lambda c, j: (0, c * group + j, 0, 0, 0)
            ),
            pl.BlockSpec((None, rank, size), lambda c, j: (0, 0, c * group + j)),
        ],
        out_shape=[
            jax.ShapeDtypeStruct(shape, BF16),
            jax.ShapeDtypeStruct((1, rank, width), BF16),
        ],
        scratch_shapes=[pltpu.VMEM((links * size + rank, tokens), BF16)],
        name="first_grad",
        **params(2),
    )(*[piece for link in ins for piece in link], proj, hidden)


def body(
    inputs, preact, handoff, first_blocks, second_blocks, left_one, right_one, left_two, right_two
):
    shape = first_blocks.shape
    links, size = shape[2], shape[-1]
    tokens, feats = inputs.shape[1:]
    count_in = feats // size
    near = count_in.bit_length()
    flips = [(1 << k) >> 1 if k < near else 0 for k in range(links)]
    spans = [slice(0, tokens // 2), slice(tokens // 2, tokens)]

    far_count = links - near - 1

    def half_sent(value):
        return [swapped(value, bit) for bit in reversed(range(1, far_count + 1))][::-1]

    ranks = left_one.shape[2]
    first_half, second_half = spans

    in_core = swapped(inputs[0], 0)
    in_one = half_sent(inputs[0, first_half])
    act, slope, proj_act = gate_call(preact, left_two, size)
    early = jnp.concatenate([nn(inputs[0], left_one[0]), proj_act], axis=1)

    upstream = after(shifted(handoff[0]), in_core, early, *in_one)
    up_core = swapped(upstream, 0)
    near_ups = [[upstream]] * near + [[up_core]]
    (second_part,) = second_call(near_ups, flips[: near + 1], act, shape, 0)
    up_shares = shares_of(UP_SHARES, far_count)
    sums, far_ups = relay(
        [cut(upstream, shares) for shares in up_shares],
        jnp.concatenate([nt(upstream, right_two[0]), early], axis=1),
        lambda stage: [second_part],
    )
    proj_grad, proj_in, proj_act = jnp.split(sums, (ranks, 2 * ranks), axis=1)

    in_two = half_sent(after(inputs[0], far_ups[-1][1])[second_half])
    hidden, *parts, back = hidden_call(
        near_ups + far_ups,
        flips,
        proj_grad,
        second_blocks,
        left_two,
        slope,
        right_one,
        first_blocks,
        near + 1,
    )
    in_sets = [[inputs[0]]] * near + [[in_core]] + [list(link) for link in zip(in_one, in_two)]
    back, *parts = lax.optimization_barrier((back, *parts, *in_two))[: 1 + len(parts)]
    found = []

    def work(stage):
        base, *beside = near_call(after(hidden, stage), first_blocks, count_in, near)
        second_grad, lefttwo_grad = second_call(
            far_ups, flips[near + 1 :], act, shape, near + 1, after(proj_grad, stage), second_part
        )
        first_grad, rightone_grad = first_call(
            in_sets, flips, after(proj_in, stage), hidden, shape
        )
        beside = jnp.concatenate([swapped(piece, 0) for piece in beside], axis=0)
        found.extend(
            [base, beside, first_grad, second_grad, rightone_grad, lefttwo_grad]
        )
        return [base, lefttwo_grad, rightone_grad]

    parts = iter(parts)
    back_links = [
        [next(parts) if share else None for share in shares]
        for shares in shares_of(BACK_SHARES, far_count)
    ]
    back_rank, far = relay(back_links, back, work)
    base, beside, first_grad, second_grad, rightone_grad, lefttwo_grad = found
    base = base + beside.astype(F32) + nt(back_rank, left_one[0])
    leftone_grad = nn(inputs[0].T, back_rank).astype(BF16)[None]
    righttwo_grad = nn(proj_act.T, upstream).astype(BF16)[None]
    total, leftone_grad, righttwo_grad = lax.optimization_barrier(
        (base, leftone_grad, righttwo_grad)
    )
    for link in far:
        total = total + jnp.concatenate(link, axis=0).astype(F32)
    input_grad = total.astype(BF16)[None]
    return (
        input_grad,
        first_grad,
        second_grad,
        leftone_grad,
        rightone_grad,
        lefttwo_grad,
        righttwo_grad,
    )


def solution(mesh):
    by_feature = P("section", None, "tensor")
    by_block = P("section", "tensor", None, None, None)
    by_row = P("section", "tensor", None)
    in_specs = (
        by_feature,
        by_feature,
        by_feature,
        by_block,
        by_block,
        by_row,
        by_feature,
        by_row,
        by_feature,
    )
    out_specs = (
        by_feature,
        by_block,
        by_block,
        by_row,
        by_feature,
        by_row,
        by_feature,
    )
    return jax.shard_map(body, mesh=mesh, in_specs=in_specs, out_specs=out_specs, check_vma=False)
```

```python
import functools

import jax
import jax.numpy as jnp
from jax import lax
from jax.experimental import pallas as pl
from jax.experimental.pallas import tpu as pltpu
from jax.sharding import PartitionSpec as P

UP_SHARES = ((2, 6, 0), (5, 3, 0))
BACK_SHARES = ((3, 5, 0), (7, 1, 0))
BF16 = jnp.bfloat16
F32 = jnp.float32


def swapped(value, bit):
    pairs = [(source, source ^ (1 << bit)) for source in range(lax.axis_size("tensor"))]
    return lax.ppermute(value, "tensor", pairs)


def shifted(value):
    peers = lax.axis_size("section")
    return lax.ppermute(value, "section", [(i, (i - 1) % peers) for i in range(peers)])


def halves(value, bit):
    half = value.shape[0] // 2
    mine = (lax.axis_index("tensor") >> bit) & 1
    keep = lax.dynamic_slice_in_dim(value, mine * half, half)
    return keep, lax.dynamic_slice_in_dim(value, (1 - mine) * half, half)


def halved(value, bit):
    keep, give = halves(value, bit)
    give = give if bit == 0 else give.astype(BF16)
    return keep + swapped(give, bit).astype(F32)


def gathered(value, bit):
    mine = (lax.axis_index("tensor") >> bit) & 1
    other = swapped(value, bit)
    first = jnp.where(mine == 0, value, other)
    second = jnp.where(mine == 0, other, value)
    return jnp.concatenate([first, second])


def shares_of(shares, count):
    return [shares[0]] * (count - 1) + [shares[1]]


def cut(value, shares):
    pieces, start = [], 0
    for share in shares:
        stop = start + value.shape[0] * share // 8
        pieces.append(value[start:stop] if share else None)
        start = stop
    return pieces


def sent(piece, bit, *others):
    return None if piece is None else swapped(after(piece, *others), bit)


def kept(pieces):
    return [piece for piece in pieces if piece is not None]


def relay(links, value, work):
    last = len(links)
    value = halved(value, 0)
    done = work(value)
    seconds = [sent(link[1], bit, done[0]) for bit, link in enumerate(links[:-1], 1)]
    if last > 1:
        keep, give = halves(value, 1)
        rows, width = links[0][0].shape
        give = give.astype(BF16)
        both = jnp.concatenate([links[0][0], give.reshape(-1, width)], axis=0)
        both = swapped(both, 1)
        firsts = [both[:rows]]
        value = keep + after(both[rows:].reshape(give.shape), *done).astype(F32)
    else:
        firsts = [sent(links[0][0], 1)]
        value = after(value, *done)
    firsts += [sent(link[0], bit) for bit, link in enumerate(links[1:], 2)]
    for bit in range(2, last):
        value = halved(value, bit)
    value = after(value, *firsts)
    seconds.append(sent(links[-1][1], last, value))
    value = (value + swapped(value.astype(BF16), last).astype(F32)).astype(BF16)
    thirds = [sent(link[2], bit, value) for bit, link in enumerate(links, 1)]
    value = after(value, *kept(seconds[:-1]))
    for bit in reversed(range(1, last)):
        value = gathered(value, bit)
    value = gathered(after(value, seconds[-1]), 0)
    return value, [kept(link) for link in zip(firsts, seconds, thirds)]


def nt(left, right):
    return lax.dot_general(left, right, (((1,), (1,)), ((), ())), preferred_element_type=F32)


def nn(left, right):
    return jnp.dot(left, right, preferred_element_type=F32)


def wide(parts):
    return parts[0] if len(parts) == 1 else jnp.concatenate(parts, axis=1)


def after(value, *others):
    return lax.optimization_barrier((value, *others))[0]


def gate_kernel(strip, preact, left_two, act, slope, proj):
    def one(r, _):
        rows = pl.ds(pl.multiple_of(r * strip, strip), strip)
        values = preact[rows, :].astype(F32)
        normal_cdf = 0.5 * (1.0 + lax.erf(values * 0.7071067811865476))
        density = jnp.exp(-0.5 * values * values) * 0.3989422804014327
        act[rows, :] = (values * normal_cdf).astype(BF16)
        slope[rows, :] = normal_cdf + values * density
        return 0

    lax.fori_loop(0, preact.shape[0] // strip, one, 0)
    term = nn(act[...], left_two[...])

    @pl.when(pl.program_id(0) == 0)
    def _():
        proj[...] = term

    @pl.when(pl.program_id(0) > 0)
    def _():
        proj[...] += term


def gate_call(preact, left_two, size):
    _, tokens, width = preact.shape
    rank = left_two.shape[2]
    return pl.pallas_call(
        functools.partial(gate_kernel, min(64, tokens)),
        grid=(width // size,),
        in_specs=[
            pl.BlockSpec((None, tokens, size), lambda i: (0, 0, i)),
            pl.BlockSpec((None, size, rank), lambda i: (0, i, 0)),
        ],
        out_specs=[
            pl.BlockSpec((tokens, size), lambda i: (0, i)),
            pl.BlockSpec((tokens, size), lambda i: (0, i)),
            pl.BlockSpec((tokens, rank), lambda i: (0, 0)),
        ],
        out_shape=[
            jax.ShapeDtypeStruct((tokens, width), BF16),
            jax.ShapeDtypeStruct((tokens, width), F32),
            jax.ShapeDtypeStruct((tokens, rank), F32),
        ],
        name="gate",
        **params(1),
    )(preact, left_two)


def params(steps):
    return dict(
        cost_estimate=pl.CostEstimate(flops=1024, bytes_accessed=1024, transcendentals=0),
        compiler_params=pltpu.CompilerParams(
            dimension_semantics=("arbitrary",) * steps, vmem_limit_bytes=56 * 2**20
        ),
    )


def taken(refs, counts):
    groups = []
    for count in counts:
        groups.append(refs[:count])
        refs = refs[count:]
    return groups, refs


def hidden_kernel(counts, part_counts, group, *refs):
    links, late = len(counts), len(part_counts)
    ups, refs = taken(refs, counts)
    proj, refs = refs[0], refs[1:]
    seconds, refs = refs[:links], refs[links:]
    left_two, slope, right_one, refs = refs[0], refs[1], refs[2], refs[3:]
    firsts, refs = refs[:late], refs[late:]
    hidden, refs = refs[0], refs[1:]
    parts, refs = taken(refs, part_counts)
    rank, up_all, hid_all = refs
    c, j = pl.program_id(0), pl.program_id(1)
    size = hidden.shape[1]

    @pl.when(j == 0)
    def _():
        for k in range(links):
            start = 0
            for piece in ups[k]:
                stop = start + piece.shape[0]
                up_all[start:stop, k * size : (k + 1) * size] = piece[...]
                start = stop
        up_all[:, links * size :] = proj[...]

    weights = wide([ref[...] for ref in seconds] + [left_two[...]])
    grad = nt(up_all[...], weights)
    hid = (grad * slope[...]).astype(BF16)
    hidden[...] = hid
    hid_all[:, pl.ds(pl.multiple_of(j * size, size), size)] = hid

    @pl.when(j == group - 1)
    def _():
        group_grad = hid_all[...]
        for n, ref in enumerate(firsts):
            part = nt(group_grad, wide([ref[g] for g in range(group)])).astype(BF16)
            start = 0
            for piece in parts[n]:
                stop = start + piece.shape[0]
                piece[...] = part[start:stop]
                start = stop
        term = nt(group_grad, right_one[...])

        @pl.when(c == 0)
        def _():
            rank[...] = term

        @pl.when(c > 0)
        def _():
            rank[...] += term


def piece_specs(sets, flips, size):
    return [
        pl.BlockSpec((piece.shape[0], size), lambda c, j, flip=flip: (0, c ^ flip))
        for pieces, flip in zip(sets, flips)
        for piece in pieces
    ]


def hidden_call(ups, flips, proj, second, left_two, slope, right_one, first, late_from):
    rows, width = slope.shape
    _, hid_count, links, size, _ = first.shape
    count_in = ups[0][0].shape[1] // size
    group = hid_count // count_in
    rank = proj.shape[1]
    late = links - late_from
    shares = [[rows * n // 8 for n in link if n] for link in shares_of(BACK_SHARES, late)]
    pieces = [n for link in shares for n in link]
    in_specs = piece_specs(ups, flips, size)
    in_specs.append(pl.BlockSpec((rows, rank), lambda c, j: (0, 0)))
    in_specs += [
        pl.BlockSpec((None, None, None, size, size), lambda c, j, k=k: (0, c * group + j, k, 0, 0))
        for k in range(links)
    ]
    in_specs.append(pl.BlockSpec((None, size, rank), lambda c, j: (0, c * group + j, 0)))
    in_specs.append(pl.BlockSpec((rows, size), lambda c, j: (0, c * group + j)))
    in_specs.append(pl.BlockSpec((None, rank, group * size), lambda c, j: (0, 0, c)))
    in_specs += [
        pl.BlockSpec((None, group, None, size, size), lambda c, j, k=k: (0, c, k, 0, 0))
        for k in range(late_from, links)
    ]
    out_specs = [pl.BlockSpec((rows, size), lambda c, j: (0, c * group + j))]
    out_specs += [pl.BlockSpec((n, size), lambda c, j: (0, c)) for n in pieces]
    out_specs.append(pl.BlockSpec((rows, rank), lambda c, j: (0, 0)))
    out_shape = [jax.ShapeDtypeStruct((rows, width), BF16)]
    out_shape += [jax.ShapeDtypeStruct((n, count_in * size), BF16) for n in pieces]
    out_shape.append(jax.ShapeDtypeStruct((rows, rank), F32))
    return pl.pallas_call(
        functools.partial(
            hidden_kernel, [len(link) for link in ups], [len(link) for link in shares], group
        ),
        grid=(count_in, group),
        in_specs=in_specs,
        out_specs=out_specs,
        out_shape=out_shape,
        scratch_shapes=[
            pltpu.VMEM((rows, links * size + rank), BF16),
            pltpu.VMEM((rows, group * size), BF16),
        ],
        name="hidden_grad",
        **params(2),
    )(
        *[piece for link in ups for piece in link], proj, *[second] * links, left_two, slope, right_one, *[first] * late
    )


def near_kernel(near, group, hid, *refs):
    weights, refs = refs[0], refs[1:]
    far_weights, base, *far, total = refs
    kk = pl.program_id(1)
    term = nt(hid[...], wide([weights[g] for g in range(group)]))

    @pl.when(kk == 0)
    def _():
        total[...] = term
        other = nt(hid[...], wide([far_weights[g] for g in range(group)])).astype(BF16)
        for m, piece in enumerate(far):
            piece[...] = other[m * piece.shape[0] : (m + 1) * piece.shape[0]]

    @pl.when(kk > 0)
    def _():
        total[...] += term

    @pl.when(kk == near - 1)
    def _():
        base[...] = total[...]


def near_call(hidden, first, count_in, near):
    rows = hidden.shape[0]
    _, hid_count, links, size, _ = first.shape
    group = hid_count // count_in

    def mate(c, kk):
        return c ^ ((1 << kk) >> 1)

    width = count_in * size
    return pl.pallas_call(
        functools.partial(near_kernel, near, group),
        grid=(count_in, near),
        in_specs=[
            pl.BlockSpec((rows, group * size), lambda c, kk: (0, mate(c, kk))),
            pl.BlockSpec(
                (None, group, None, size, size), lambda c, kk: (0, mate(c, kk), kk, 0, 0)
            ),
            pl.BlockSpec((None, group, None, size, size), lambda c, kk: (0, c, near, 0, 0)),
        ],
        out_specs=[
            pl.BlockSpec((rows, size), lambda c, kk: (0, c)),
            *[pl.BlockSpec((rows // 2, size), lambda c, kk: (0, c))] * 2,
        ],
        out_shape=[
            jax.ShapeDtypeStruct((rows, width), F32),
            *[jax.ShapeDtypeStruct((rows // 2, width), BF16)] * 2,
        ],
        scratch_shapes=[pltpu.VMEM((rows, size), F32)],
        name="near_parts",
        **params(2),
    )(hidden, first, first)


def second_kernel(counts, group, has_proj, *refs):
    count = len(counts)
    ups, refs = taken(refs, counts)
    if has_proj:
        proj, act, _, out, left_two, turned = refs
    else:
        act, out, turned = refs
    k = pl.program_id(1)
    size = ups[0][0].shape[1]

    @pl.when(k == 0)
    def _():
        for g in range(group):
            turned[g * size : (g + 1) * size, :] = act[:, g * size : (g + 1) * size].T

    def store(pieces):
        up = jnp.concatenate([piece[...] for piece in pieces], axis=0)
        grads = nn(turned[...], up).astype(BF16)
        for g in range(group):
            out[g] = grads[g * size : (g + 1) * size]

    for n in range(count):
        pl.when(k == n)(lambda n=n: store(ups[n]))

    if has_proj:

        @pl.when(k == count - 1)
        def _():
            left_two[...] = nn(turned[...], proj[...]).astype(BF16)


def second_call(ups, flips, act, shape, start, proj=None, partial=None):
    count = len(ups)
    tokens = act.shape[0]
    _, hid_count, links, size, _ = shape
    count_in = ups[0][0].shape[1] // size
    group = hid_count // count_in
    has_proj = proj is not None
    in_specs = piece_specs(ups, flips, size)
    args = [piece for link in ups for piece in link]
    out_specs = [
        pl.BlockSpec((None, group, None, size, size), lambda c, k: (0, c, start + k, 0, 0))
    ]
    out_shape = [jax.ShapeDtypeStruct(shape, BF16)]
    aliases = {}
    if has_proj:
        rank = proj.shape[1]
        in_specs.append(pl.BlockSpec((tokens, rank), lambda c, k: (0, 0)))
        args.append(proj)
        out_specs.append(pl.BlockSpec((None, group * size, rank), lambda c, k: (0, c, 0)))
        out_shape.append(jax.ShapeDtypeStruct((1, hid_count * size, rank), BF16))
    in_specs.append(pl.BlockSpec((tokens, group * size), lambda c, k: (0, c)))
    args.append(act)
    if has_proj:
        in_specs.append(pl.BlockSpec(memory_space=pl.ANY))
        args.append(partial)
        aliases = {len(args) - 1: 0}
    return pl.pallas_call(
        functools.partial(second_kernel, [len(link) for link in ups], group, has_proj),
        grid=(count_in, count),
        in_specs=in_specs,
        out_specs=out_specs,
        out_shape=out_shape,
        scratch_shapes=[pltpu.VMEM((group * size, tokens), BF16)],
        input_output_aliases=aliases,
        name="second_late" if has_proj else "second_early",
        **params(2),
    )(*args)


def first_kernel(counts, *refs):
    links = len(counts)
    ins, refs = taken(refs, counts)
    proj, hid, out, right_one, in_all = refs
    size = hid.shape[1]

    @pl.when(pl.program_id(1) == 0)
    def _():
        for k in range(links):
            start = 0
            for piece in ins[k]:
                stop = start + piece.shape[0]
                in_all[k * size : (k + 1) * size, start:stop] = piece[...].T
                start = stop
        in_all[links * size :, :] = proj[...].T

    grads = nn(in_all[...], hid[...]).astype(BF16)
    for k in range(links):
        out[k] = grads[k * size : (k + 1) * size]
    right_one[...] = grads[links * size :]


def first_call(ins, flips, proj, hidden, shape):
    tokens, width = hidden.shape
    _, hid_count, links, size, _ = shape
    count_in = ins[0][0].shape[1] // size
    group = hid_count // count_in
    rank = proj.shape[1]
    in_specs = piece_specs(ins, flips, size)
    in_specs.append(pl.BlockSpec((tokens, rank), lambda c, j: (0, 0)))
    in_specs.append(pl.BlockSpec((tokens, size), lambda c, j: (0, c * group + j)))
    return pl.pallas_call(
        functools.partial(first_kernel, [len(link) for link in ins]),
        grid=(count_in, group),
        in_specs=in_specs,
        out_specs=[
            pl.BlockSpec(
                (None, None, links, size, size), lambda c, j: (0, c * group + j, 0, 0, 0)
            ),
            pl.BlockSpec((None, rank, size), lambda c, j: (0, 0, c * group + j)),
        ],
        out_shape=[
            jax.ShapeDtypeStruct(shape, BF16),
            jax.ShapeDtypeStruct((1, rank, width), BF16),
        ],
        scratch_shapes=[pltpu.VMEM((links * size + rank, tokens), BF16)],
        name="first_grad",
        **params(2),
    )(*[piece for link in ins for piece in link], proj, hidden)


def body(
    inputs, preact, handoff, first_blocks, second_blocks, left_one, right_one, left_two, right_two
):
    shape = first_blocks.shape
    links, size = shape[2], shape[-1]
    tokens, feats = inputs.shape[1:]
    count_in = feats // size
    near = count_in.bit_length()
    flips = [(1 << k) >> 1 if k < near else 0 for k in range(links)]
    spans = [slice(0, tokens // 2), slice(tokens // 2, tokens)]

    far_count = links - near - 1

    def half_sent(value):
        return [swapped(value, bit) for bit in reversed(range(1, far_count + 1))][::-1]

    ranks = left_one.shape[2]
    first_half, second_half = spans

    in_core = swapped(inputs[0], 0)
    in_one = half_sent(inputs[0, first_half])
    act, slope, proj_act = gate_call(preact, left_two, size)
    early = jnp.concatenate([nn(inputs[0], left_one[0]), proj_act], axis=1)

    upstream = after(shifted(handoff[0]), in_core, early, *in_one)
    up_core = swapped(upstream, 0)
    near_ups = [[upstream]] * near + [[up_core]]
    (second_part,) = second_call(near_ups, flips[: near + 1], act, shape, 0)
    up_shares = shares_of(UP_SHARES, far_count)
    sums, far_ups = relay(
        [cut(upstream, shares) for shares in up_shares],
        jnp.concatenate([nt(upstream, right_two[0]), early], axis=1),
        lambda stage: [second_part],
    )
    proj_grad, proj_in, proj_act = jnp.split(sums, (ranks, 2 * ranks), axis=1)

    in_two = half_sent(after(inputs[0], far_ups[-1][1])[second_half])
    hidden, *parts, back = hidden_call(
        near_ups + far_ups,
        flips,
        proj_grad,
        second_blocks,
        left_two,
        slope,
        right_one,
        first_blocks,
        near + 1,
    )
    in_sets = [[inputs[0]]] * near + [[in_core]] + [list(link) for link in zip(in_one, in_two)]
    back, *parts = lax.optimization_barrier((back, *parts, *in_two))[: 1 + len(parts)]
    found = []

    def work(stage):
        base, *beside = near_call(after(hidden, stage), first_blocks, count_in, near)
        second_grad, lefttwo_grad = second_call(
            far_ups, flips[near + 1 :], act, shape, near + 1, after(proj_grad, stage), second_part
        )
        first_grad, rightone_grad = first_call(
            in_sets, flips, after(proj_in, stage), hidden, shape
        )
        beside = jnp.concatenate([swapped(piece, 0) for piece in beside], axis=0)
        found.extend(
            [base, beside, first_grad, second_grad, rightone_grad, lefttwo_grad]
        )
        return [base, lefttwo_grad, rightone_grad]

    parts = iter(parts)
    back_links = [
        [next(parts) if share else None for share in shares]
        for shares in shares_of(BACK_SHARES, far_count)
    ]
    back_rank, far = relay(back_links, back, work)
    base, beside, first_grad, second_grad, rightone_grad, lefttwo_grad = found
    base = base + beside.astype(F32) + nt(back_rank, left_one[0])
    leftone_grad = nn(inputs[0].T, back_rank).astype(BF16)[None]
    righttwo_grad = nn(proj_act.T, upstream).astype(BF16)[None]
    total, leftone_grad, righttwo_grad = lax.optimization_barrier(
        (base, leftone_grad, righttwo_grad)
    )
    for link in far:
        total = total + jnp.concatenate(link, axis=0).astype(F32)
    input_grad = total.astype(BF16)[None]
    return (
        input_grad,
        first_grad,
        second_grad,
        leftone_grad,
        rightone_grad,
        lefttwo_grad,
        righttwo_grad,
    )


def solution(mesh):
    by_feature = P("section", None, "tensor")
    by_block = P("section", "tensor", None, None, None)
    by_row = P("section", "tensor", None)
    in_specs = (
        by_feature,
        by_feature,
        by_feature,
        by_block,
        by_block,
        by_row,
        by_feature,
        by_row,
        by_feature,
    )
    out_specs = (
        by_feature,
        by_block,
        by_block,
        by_row,
        by_feature,
        by_row,
        by_feature,
    )
    return jax.shard_map(body, mesh=mesh, in_specs=in_specs, out_specs=out_specs, check_vma=False)
```

```python
import functools

import jax
import jax.numpy as jnp
from jax import lax
from jax.experimental import pallas as pl
from jax.experimental.pallas import tpu as pltpu
from jax.sharding import PartitionSpec as P

UP_SHARES = ((2, 6, 0), (5, 3, 0))
BACK_SHARES = ((3, 5, 0), (7, 1, 0))
BF16 = jnp.bfloat16
F32 = jnp.float32


def swapped(value, bit):
    pairs = [(source, source ^ (1 << bit)) for source in range(lax.axis_size("tensor"))]
    return lax.ppermute(value, "tensor", pairs)


def shifted(value):
    peers = lax.axis_size("section")
    return lax.ppermute(value, "section", [(i, (i - 1) % peers) for i in range(peers)])


def halves(value, bit):
    half = value.shape[0] // 2
    mine = (lax.axis_index("tensor") >> bit) & 1
    keep = lax.dynamic_slice_in_dim(value, mine * half, half)
    return keep, lax.dynamic_slice_in_dim(value, (1 - mine) * half, half)


def halved(value, bit):
    keep, give = halves(value, bit)
    give = give if bit == 0 else give.astype(BF16)
    return keep + swapped(give, bit).astype(F32)


def gathered(value, bit):
    mine = (lax.axis_index("tensor") >> bit) & 1
    other = swapped(value, bit)
    first = jnp.where(mine == 0, value, other)
    second = jnp.where(mine == 0, other, value)
    return jnp.concatenate([first, second])


def shares_of(shares, count):
    return [shares[0]] * (count - 1) + [shares[1]]


def cut(value, shares):
    pieces, start = [], 0
    for share in shares:
        stop = start + value.shape[0] * share // 8
        pieces.append(value[start:stop] if share else None)
        start = stop
    return pieces


def sent(piece, bit, *others):
    return None if piece is None else swapped(after(piece, *others), bit)


def kept(pieces):
    return [piece for piece in pieces if piece is not None]


def relay(links, value, work):
    last = len(links)
    value = halved(value, 0)
    done = work(value)
    seconds = [sent(link[1], bit, done[0]) for bit, link in enumerate(links[:-1], 1)]
    if last > 1:
        keep, give = halves(value, 1)
        rows, width = links[0][0].shape
        give = give.astype(BF16)
        both = jnp.concatenate([links[0][0], give.reshape(-1, width)], axis=0)
        both = swapped(both, 1)
        firsts = [both[:rows]]
        value = keep + after(both[rows:].reshape(give.shape), *done).astype(F32)
    else:
        firsts = [sent(links[0][0], 1)]
        value = after(value, *done)
    firsts += [sent(link[0], bit) for bit, link in enumerate(links[1:], 2)]
    for bit in range(2, last):
        value = halved(value, bit)
    value = after(value, *firsts)
    seconds.append(sent(links[-1][1], last, value))
    value = (value + swapped(value.astype(BF16), last).astype(F32)).astype(BF16)
    thirds = [sent(link[2], bit, value) for bit, link in enumerate(links, 1)]
    value = after(value, *kept(seconds))
    for bit in reversed(range(1, last)):
        value = gathered(value, bit)
    return gathered(value, 0), value, [kept(link) for link in zip(firsts, seconds, thirds)]


def nt(left, right):
    return lax.dot_general(left, right, (((1,), (1,)), ((), ())), preferred_element_type=F32)


def nn(left, right):
    return jnp.dot(left, right, preferred_element_type=F32)


def wide(parts):
    return parts[0] if len(parts) == 1 else jnp.concatenate(parts, axis=1)


def after(value, *others):
    return lax.optimization_barrier((value, *others))[0]


def gate_kernel(strip, preact, left_two, act, slope, proj):
    def one(r, _):
        rows = pl.ds(pl.multiple_of(r * strip, strip), strip)
        values = preact[rows, :].astype(F32)
        normal_cdf = 0.5 * (1.0 + lax.erf(values * 0.7071067811865476))
        density = jnp.exp(-0.5 * values * values) * 0.3989422804014327
        act[rows, :] = (values * normal_cdf).astype(BF16)
        slope[rows, :] = normal_cdf + values * density
        return 0

    lax.fori_loop(0, preact.shape[0] // strip, one, 0)
    term = nn(act[...], left_two[...])

    @pl.when(pl.program_id(0) == 0)
    def _():
        proj[...] = term

    @pl.when(pl.program_id(0) > 0)
    def _():
        proj[...] += term


def gate_call(preact, left_two, size):
    _, tokens, width = preact.shape
    rank = left_two.shape[2]
    return pl.pallas_call(
        functools.partial(gate_kernel, min(64, tokens)),
        grid=(width // size,),
        in_specs=[
            pl.BlockSpec((None, tokens, size), lambda i: (0, 0, i)),
            pl.BlockSpec((None, size, rank), lambda i: (0, i, 0)),
        ],
        out_specs=[
            pl.BlockSpec((tokens, size), lambda i: (0, i)),
            pl.BlockSpec((tokens, size), lambda i: (0, i)),
            pl.BlockSpec((tokens, rank), lambda i: (0, 0)),
        ],
        out_shape=[
            jax.ShapeDtypeStruct((tokens, width), BF16),
            jax.ShapeDtypeStruct((tokens, width), F32),
            jax.ShapeDtypeStruct((tokens, rank), F32),
        ],
        name="gate",
        **params(1),
    )(preact, left_two)


def params(steps):
    return dict(
        cost_estimate=pl.CostEstimate(flops=1024, bytes_accessed=1024, transcendentals=0),
        compiler_params=pltpu.CompilerParams(
            dimension_semantics=("arbitrary",) * steps, vmem_limit_bytes=56 * 2**20
        ),
    )


def taken(refs, counts):
    groups = []
    for count in counts:
        groups.append(refs[:count])
        refs = refs[count:]
    return groups, refs


def hidden_kernel(counts, part_counts, group, *refs):
    links, late = len(counts), len(part_counts)
    ups, refs = taken(refs, counts)
    proj, refs = refs[0], refs[1:]
    seconds, refs = refs[:links], refs[links:]
    left_two, slope, right_one, refs = refs[0], refs[1], refs[2], refs[3:]
    firsts, refs = refs[:late], refs[late:]
    hidden, refs = refs[0], refs[1:]
    parts, refs = taken(refs, part_counts)
    rank, up_all, hid_all = refs
    c, j = pl.program_id(0), pl.program_id(1)
    size = hidden.shape[1]

    @pl.when(j == 0)
    def _():
        for k in range(links):
            start = 0
            for piece in ups[k]:
                stop = start + piece.shape[0]
                up_all[start:stop, k * size : (k + 1) * size] = piece[...]
                start = stop
        up_all[:, links * size :] = proj[...]

    weights = wide([ref[...] for ref in seconds] + [left_two[...]])
    grad = nt(up_all[...], weights)
    hid = (grad * slope[...]).astype(BF16)
    hidden[...] = hid
    hid_all[:, pl.ds(pl.multiple_of(j * size, size), size)] = hid

    @pl.when(j == group - 1)
    def _():
        group_grad = hid_all[...]
        for n, ref in enumerate(firsts):
            part = nt(group_grad, wide([ref[g] for g in range(group)])).astype(BF16)
            start = 0
            for piece in parts[n]:
                stop = start + piece.shape[0]
                piece[...] = part[start:stop]
                start = stop
        term = nt(group_grad, right_one[...])

        @pl.when(c == 0)
        def _():
            rank[...] = term

        @pl.when(c > 0)
        def _():
            rank[...] += term


def piece_specs(sets, flips, size):
    return [
        pl.BlockSpec((piece.shape[0], size), lambda c, j, flip=flip: (0, c ^ flip))
        for pieces, flip in zip(sets, flips)
        for piece in pieces
    ]


def hidden_call(ups, flips, proj, second, left_two, slope, right_one, first, late_from):
    rows, width = slope.shape
    _, hid_count, links, size, _ = first.shape
    count_in = ups[0][0].shape[1] // size
    group = hid_count // count_in
    rank = proj.shape[1]
    late = links - late_from
    shares = [[rows * n // 8 for n in link if n] for link in shares_of(BACK_SHARES, late)]
    pieces = [n for link in shares for n in link]
    in_specs = piece_specs(ups, flips, size)
    in_specs.append(pl.BlockSpec((rows, rank), lambda c, j: (0, 0)))
    in_specs += [
        pl.BlockSpec((None, None, None, size, size), lambda c, j, k=k: (0, c * group + j, k, 0, 0))
        for k in range(links)
    ]
    in_specs.append(pl.BlockSpec((None, size, rank), lambda c, j: (0, c * group + j, 0)))
    in_specs.append(pl.BlockSpec((rows, size), lambda c, j: (0, c * group + j)))
    in_specs.append(pl.BlockSpec((None, rank, group * size), lambda c, j: (0, 0, c)))
    in_specs += [
        pl.BlockSpec((None, group, None, size, size), lambda c, j, k=k: (0, c, k, 0, 0))
        for k in range(late_from, links)
    ]
    out_specs = [pl.BlockSpec((rows, size), lambda c, j: (0, c * group + j))]
    out_specs += [pl.BlockSpec((n, size), lambda c, j: (0, c)) for n in pieces]
    out_specs.append(pl.BlockSpec((rows, rank), lambda c, j: (0, 0)))
    out_shape = [jax.ShapeDtypeStruct((rows, width), BF16)]
    out_shape += [jax.ShapeDtypeStruct((n, count_in * size), BF16) for n in pieces]
    out_shape.append(jax.ShapeDtypeStruct((rows, rank), F32))
    return pl.pallas_call(
        functools.partial(
            hidden_kernel, [len(link) for link in ups], [len(link) for link in shares], group
        ),
        grid=(count_in, group),
        in_specs=in_specs,
        out_specs=out_specs,
        out_shape=out_shape,
        scratch_shapes=[
            pltpu.VMEM((rows, links * size + rank), BF16),
            pltpu.VMEM((rows, group * size), BF16),
        ],
        name="hidden_grad",
        **params(2),
    )(
        *[piece for link in ups for piece in link], proj, *[second] * links, left_two, slope, right_one, *[first] * late
    )


def near_kernel(near, group, hid, *refs):
    weights, refs = refs[0], refs[1:]
    far_weights, base, *far, total = refs
    kk = pl.program_id(1)
    term = nt(hid[...], wide([weights[g] for g in range(group)]))

    @pl.when(kk == 0)
    def _():
        total[...] = term
        other = nt(hid[...], wide([far_weights[g] for g in range(group)])).astype(BF16)
        for m, piece in enumerate(far):
            piece[...] = other[m * piece.shape[0] : (m + 1) * piece.shape[0]]

    @pl.when(kk > 0)
    def _():
        total[...] += term

    @pl.when(kk == near - 1)
    def _():
        base[...] = total[...]


def near_call(hidden, first, count_in, near):
    rows = hidden.shape[0]
    _, hid_count, links, size, _ = first.shape
    group = hid_count // count_in

    def mate(c, kk):
        return c ^ ((1 << kk) >> 1)

    width = count_in * size
    return pl.pallas_call(
        functools.partial(near_kernel, near, group),
        grid=(count_in, near),
        in_specs=[
            pl.BlockSpec((rows, group * size), lambda c, kk: (0, mate(c, kk))),
            pl.BlockSpec(
                (None, group, None, size, size), lambda c, kk: (0, mate(c, kk), kk, 0, 0)
            ),
            pl.BlockSpec((None, group, None, size, size), lambda c, kk: (0, c, near, 0, 0)),
        ],
        out_specs=[
            pl.BlockSpec((rows, size), lambda c, kk: (0, c)),
            *[pl.BlockSpec((rows // 2, size), lambda c, kk: (0, c))] * 2,
        ],
        out_shape=[
            jax.ShapeDtypeStruct((rows, width), F32),
            *[jax.ShapeDtypeStruct((rows // 2, width), BF16)] * 2,
        ],
        scratch_shapes=[pltpu.VMEM((rows, size), F32)],
        name="near_parts",
        **params(2),
    )(hidden, first, first)


def second_kernel(counts, group, has_proj, *refs):
    count = len(counts)
    ups, refs = taken(refs, counts)
    if has_proj:
        proj, act, _, out, left_two, turned = refs
    else:
        act, out, turned = refs
    k = pl.program_id(1)
    size = ups[0][0].shape[1]

    @pl.when(k == 0)
    def _():
        for g in range(group):
            turned[g * size : (g + 1) * size, :] = act[:, g * size : (g + 1) * size].T

    def store(pieces):
        up = jnp.concatenate([piece[...] for piece in pieces], axis=0)
        grads = nn(turned[...], up).astype(BF16)
        for g in range(group):
            out[g] = grads[g * size : (g + 1) * size]

    for n in range(count):
        pl.when(k == n)(lambda n=n: store(ups[n]))

    if has_proj:

        @pl.when(k == count - 1)
        def _():
            left_two[...] = nn(turned[...], proj[...]).astype(BF16)


def second_call(ups, flips, act, shape, start, proj=None, partial=None):
    count = len(ups)
    tokens = act.shape[0]
    _, hid_count, links, size, _ = shape
    count_in = ups[0][0].shape[1] // size
    group = hid_count // count_in
    has_proj = proj is not None
    in_specs = piece_specs(ups, flips, size)
    args = [piece for link in ups for piece in link]
    out_specs = [
        pl.BlockSpec((None, group, None, size, size), lambda c, k: (0, c, start + k, 0, 0))
    ]
    out_shape = [jax.ShapeDtypeStruct(shape, BF16)]
    aliases = {}
    if has_proj:
        rank = proj.shape[1]
        in_specs.append(pl.BlockSpec((tokens, rank), lambda c, k: (0, 0)))
        args.append(proj)
        out_specs.append(pl.BlockSpec((None, group * size, rank), lambda c, k: (0, c, 0)))
        out_shape.append(jax.ShapeDtypeStruct((1, hid_count * size, rank), BF16))
    in_specs.append(pl.BlockSpec((tokens, group * size), lambda c, k: (0, c)))
    args.append(act)
    if has_proj:
        in_specs.append(pl.BlockSpec(memory_space=pl.ANY))
        args.append(partial)
        aliases = {len(args) - 1: 0}
    return pl.pallas_call(
        functools.partial(second_kernel, [len(link) for link in ups], group, has_proj),
        grid=(count_in, count),
        in_specs=in_specs,
        out_specs=out_specs,
        out_shape=out_shape,
        scratch_shapes=[pltpu.VMEM((group * size, tokens), BF16)],
        input_output_aliases=aliases,
        name="second_late" if has_proj else "second_early",
        **params(2),
    )(*args)


def first_kernel(counts, *refs):
    links = len(counts)
    ins, refs = taken(refs, counts)
    proj, hid, out, right_one, in_all = refs
    size = hid.shape[1]

    @pl.when(pl.program_id(1) == 0)
    def _():
        for k in range(links):
            start = 0
            for piece in ins[k]:
                stop = start + piece.shape[0]
                in_all[k * size : (k + 1) * size, start:stop] = piece[...].T
                start = stop
        in_all[links * size :, :] = proj[...].T

    grads = nn(in_all[...], hid[...]).astype(BF16)
    for k in range(links):
        out[k] = grads[k * size : (k + 1) * size]
    right_one[...] = grads[links * size :]


def first_call(ins, flips, proj, hidden, shape):
    tokens, width = hidden.shape
    _, hid_count, links, size, _ = shape
    count_in = ins[0][0].shape[1] // size
    group = hid_count // count_in
    rank = proj.shape[1]
    in_specs = piece_specs(ins, flips, size)
    in_specs.append(pl.BlockSpec((tokens, rank), lambda c, j: (0, 0)))
    in_specs.append(pl.BlockSpec((tokens, size), lambda c, j: (0, c * group + j)))
    return pl.pallas_call(
        functools.partial(first_kernel, [len(link) for link in ins]),
        grid=(count_in, group),
        in_specs=in_specs,
        out_specs=[
            pl.BlockSpec(
                (None, None, links, size, size), lambda c, j: (0, c * group + j, 0, 0, 0)
            ),
            pl.BlockSpec((None, rank, size), lambda c, j: (0, 0, c * group + j)),
        ],
        out_shape=[
            jax.ShapeDtypeStruct(shape, BF16),
            jax.ShapeDtypeStruct((1, rank, width), BF16),
        ],
        scratch_shapes=[pltpu.VMEM((links * size + rank, tokens), BF16)],
        name="first_grad",
        **params(2),
    )(*[piece for link in ins for piece in link], proj, hidden)


def body(
    inputs, preact, handoff, first_blocks, second_blocks, left_one, right_one, left_two, right_two
):
    shape = first_blocks.shape
    links, size = shape[2], shape[-1]
    tokens, feats = inputs.shape[1:]
    count_in = feats // size
    near = count_in.bit_length()
    flips = [(1 << k) >> 1 if k < near else 0 for k in range(links)]
    spans = [slice(0, tokens // 2), slice(tokens // 2, tokens)]

    far_count = links - near - 1

    def half_sent(value):
        return [swapped(value, bit) for bit in reversed(range(1, far_count + 1))][::-1]

    ranks = left_one.shape[2]
    first_half, second_half = spans

    in_core = swapped(inputs[0], 0)
    in_one = half_sent(inputs[0, first_half])
    act, slope, proj_act = gate_call(preact, left_two, size)
    early = jnp.concatenate([nn(inputs[0], left_one[0]), proj_act], axis=1)

    upstream = after(shifted(handoff[0]), in_core, early, *in_one)
    up_core = swapped(upstream, 0)
    near_ups = [[upstream]] * near + [[up_core]]
    (second_part,) = second_call(near_ups, flips[: near + 1], act, shape, 0)
    up_shares = shares_of(UP_SHARES, far_count)
    sums, stage, far_ups = relay(
        [cut(upstream, shares) for shares in up_shares],
        jnp.concatenate([nt(upstream, right_two[0]), early], axis=1),
        lambda stage: [second_part],
    )
    proj_grad, proj_in, proj_act = jnp.split(sums, (ranks, 2 * ranks), axis=1)

    in_two = [
        swapped(after(inputs[0], far_ups[-1][1] if bit == far_count else stage)[second_half], bit)
        for bit in range(1, far_count + 1)
    ]
    hidden, *parts, back = hidden_call(
        near_ups + far_ups,
        flips,
        proj_grad,
        second_blocks,
        left_two,
        slope,
        right_one,
        first_blocks,
        near + 1,
    )
    in_sets = [[inputs[0]]] * near + [[in_core]] + [list(link) for link in zip(in_one, in_two)]
    back, *parts = lax.optimization_barrier((back, *parts, *in_two))[: 1 + len(parts)]
    found = []

    def work(stage):
        base, *beside = near_call(after(hidden, stage), first_blocks, count_in, near)
        second_grad, lefttwo_grad = second_call(
            far_ups, flips[near + 1 :], act, shape, near + 1, after(proj_grad, stage), second_part
        )
        first_grad, rightone_grad = first_call(
            in_sets, flips, after(proj_in, stage), hidden, shape
        )
        beside = jnp.concatenate([swapped(piece, 0) for piece in beside], axis=0)
        found.extend(
            [base, beside, first_grad, second_grad, rightone_grad, lefttwo_grad]
        )
        return [base, lefttwo_grad, rightone_grad]

    parts = iter(parts)
    back_links = [
        [next(parts) if share else None for share in shares]
        for shares in shares_of(BACK_SHARES, far_count)
    ]
    back_rank, _, far = relay(back_links, back, work)
    base, beside, first_grad, second_grad, rightone_grad, lefttwo_grad = found
    base = base + beside.astype(F32) + nt(back_rank, left_one[0])
    leftone_grad = nn(inputs[0].T, back_rank).astype(BF16)[None]
    righttwo_grad = nn(proj_act.T, upstream).astype(BF16)[None]
    total, leftone_grad, righttwo_grad = lax.optimization_barrier(
        (base, leftone_grad, righttwo_grad)
    )
    for link in far:
        total = total + jnp.concatenate(link, axis=0).astype(F32)
    input_grad = total.astype(BF16)[None]
    return (
        input_grad,
        first_grad,
        second_grad,
        leftone_grad,
        rightone_grad,
        lefttwo_grad,
        righttwo_grad,
    )


def solution(mesh):
    by_feature = P("section", None, "tensor")
    by_block = P("section", "tensor", None, None, None)
    by_row = P("section", "tensor", None)
    in_specs = (
        by_feature,
        by_feature,
        by_feature,
        by_block,
        by_block,
        by_row,
        by_feature,
        by_row,
        by_feature,
    )
    out_specs = (
        by_feature,
        by_block,
        by_block,
        by_row,
        by_feature,
        by_row,
        by_feature,
    )
    return jax.shard_map(body, mesh=mesh, in_specs=in_specs, out_specs=out_specs, check_vma=False)
```

```python
import functools

import jax
import jax.numpy as jnp
from jax import lax
from jax.experimental import pallas as pl
from jax.experimental.pallas import tpu as pltpu
from jax.sharding import PartitionSpec as P

UP_SHARES = ((2, 6, 0), (5, 3, 0))
BACK_SHARES = ((3, 4, 1), (7, 1, 0))
BF16 = jnp.bfloat16
F32 = jnp.float32


def swapped(value, bit):
    pairs = [(source, source ^ (1 << bit)) for source in range(lax.axis_size("tensor"))]
    return lax.ppermute(value, "tensor", pairs)


def shifted(value):
    peers = lax.axis_size("section")
    return lax.ppermute(value, "section", [(i, (i - 1) % peers) for i in range(peers)])


def halves(value, bit):
    half = value.shape[0] // 2
    mine = (lax.axis_index("tensor") >> bit) & 1
    keep = lax.dynamic_slice_in_dim(value, mine * half, half)
    return keep, lax.dynamic_slice_in_dim(value, (1 - mine) * half, half)


def halved(value, bit):
    keep, give = halves(value, bit)
    give = give if bit == 0 else give.astype(BF16)
    return keep + swapped(give, bit).astype(F32)


def gathered(value, bit):
    mine = (lax.axis_index("tensor") >> bit) & 1
    other = swapped(value, bit)
    first = jnp.where(mine == 0, value, other)
    second = jnp.where(mine == 0, other, value)
    return jnp.concatenate([first, second])


def shares_of(shares, count):
    return [shares[0]] * (count - 1) + [shares[1]]


def cut(value, shares):
    pieces, start = [], 0
    for share in shares:
        stop = start + value.shape[0] * share // 8
        pieces.append(value[start:stop] if share else None)
        start = stop
    return pieces


def sent(piece, bit, *others):
    return None if piece is None else swapped(after(piece, *others), bit)


def kept(pieces):
    return [piece for piece in pieces if piece is not None]


def relay(links, value, work):
    last = len(links)
    value = halved(value, 0)
    done = work(value)
    seconds = [sent(link[1], bit, done[0]) for bit, link in enumerate(links[:-1], 1)]
    if last > 1:
        keep, give = halves(value, 1)
        rows, width = links[0][0].shape
        give = give.astype(BF16)
        both = jnp.concatenate([links[0][0], give.reshape(-1, width)], axis=0)
        both = swapped(both, 1)
        firsts = [both[:rows]]
        value = keep + after(both[rows:].reshape(give.shape), *done).astype(F32)
    else:
        firsts = [sent(links[0][0], 1)]
        value = after(value, *done)
    firsts += [sent(link[0], bit) for bit, link in enumerate(links[1:], 2)]
    for bit in range(2, last):
        value = halved(value, bit)
    value = after(value, *firsts)
    seconds.append(sent(links[-1][1], last, value))
    value = (value + swapped(value.astype(BF16), last).astype(F32)).astype(BF16)
    thirds = [sent(link[2], bit, value) for bit, link in enumerate(links, 1)]
    value = after(value, *kept(seconds))
    for bit in reversed(range(1, last)):
        value = gathered(value, bit)
    return gathered(value, 0), value, [kept(link) for link in zip(firsts, seconds, thirds)]


def nt(left, right):
    return lax.dot_general(left, right, (((1,), (1,)), ((), ())), preferred_element_type=F32)


def nn(left, right):
    return jnp.dot(left, right, preferred_element_type=F32)


def wide(parts):
    return parts[0] if len(parts) == 1 else jnp.concatenate(parts, axis=1)


def after(value, *others):
    return lax.optimization_barrier((value, *others))[0]


def gate_kernel(strip, preact, left_two, act, slope, proj):
    def one(r, _):
        rows = pl.ds(pl.multiple_of(r * strip, strip), strip)
        values = preact[rows, :].astype(F32)
        normal_cdf = 0.5 * (1.0 + lax.erf(values * 0.7071067811865476))
        density = jnp.exp(-0.5 * values * values) * 0.3989422804014327
        act[rows, :] = (values * normal_cdf).astype(BF16)
        slope[rows, :] = normal_cdf + values * density
        return 0

    lax.fori_loop(0, preact.shape[0] // strip, one, 0)
    term = nn(act[...], left_two[...])

    @pl.when(pl.program_id(0) == 0)
    def _():
        proj[...] = term

    @pl.when(pl.program_id(0) > 0)
    def _():
        proj[...] += term


def gate_call(preact, left_two, size):
    _, tokens, width = preact.shape
    rank = left_two.shape[2]
    return pl.pallas_call(
        functools.partial(gate_kernel, min(64, tokens)),
        grid=(width // size,),
        in_specs=[
            pl.BlockSpec((None, tokens, size), lambda i: (0, 0, i)),
            pl.BlockSpec((None, size, rank), lambda i: (0, i, 0)),
        ],
        out_specs=[
            pl.BlockSpec((tokens, size), lambda i: (0, i)),
            pl.BlockSpec((tokens, size), lambda i: (0, i)),
            pl.BlockSpec((tokens, rank), lambda i: (0, 0)),
        ],
        out_shape=[
            jax.ShapeDtypeStruct((tokens, width), BF16),
            jax.ShapeDtypeStruct((tokens, width), F32),
            jax.ShapeDtypeStruct((tokens, rank), F32),
        ],
        name="gate",
        **params(1),
    )(preact, left_two)


def params(steps):
    return dict(
        cost_estimate=pl.CostEstimate(flops=1024, bytes_accessed=1024, transcendentals=0),
        compiler_params=pltpu.CompilerParams(
            dimension_semantics=("arbitrary",) * steps, vmem_limit_bytes=56 * 2**20
        ),
    )


def taken(refs, counts):
    groups = []
    for count in counts:
        groups.append(refs[:count])
        refs = refs[count:]
    return groups, refs


def hidden_kernel(counts, part_counts, group, *refs):
    links, late = len(counts), len(part_counts)
    ups, refs = taken(refs, counts)
    proj, refs = refs[0], refs[1:]
    seconds, refs = refs[:links], refs[links:]
    left_two, slope, right_one, refs = refs[0], refs[1], refs[2], refs[3:]
    firsts, refs = refs[:late], refs[late:]
    hidden, refs = refs[0], refs[1:]
    parts, refs = taken(refs, part_counts)
    rank, up_all, hid_all = refs
    c, j = pl.program_id(0), pl.program_id(1)
    size = hidden.shape[1]

    @pl.when(j == 0)
    def _():
        for k in range(links):
            start = 0
            for piece in ups[k]:
                stop = start + piece.shape[0]
                up_all[start:stop, k * size : (k + 1) * size] = piece[...]
                start = stop
        up_all[:, links * size :] = proj[...]

    weights = wide([ref[...] for ref in seconds] + [left_two[...]])
    grad = nt(up_all[...], weights)
    hid = (grad * slope[...]).astype(BF16)
    hidden[...] = hid
    hid_all[:, pl.ds(pl.multiple_of(j * size, size), size)] = hid

    @pl.when(j == group - 1)
    def _():
        group_grad = hid_all[...]
        for n, ref in enumerate(firsts):
            part = nt(group_grad, wide([ref[g] for g in range(group)])).astype(BF16)
            start = 0
            for piece in parts[n]:
                stop = start + piece.shape[0]
                piece[...] = part[start:stop]
                start = stop
        term = nt(group_grad, right_one[...])

        @pl.when(c == 0)
        def _():
            rank[...] = term

        @pl.when(c > 0)
        def _():
            rank[...] += term


def piece_specs(sets, flips, size):
    return [
        pl.BlockSpec((piece.shape[0], size), lambda c, j, flip=flip: (0, c ^ flip))
        for pieces, flip in zip(sets, flips)
        for piece in pieces
    ]


def hidden_call(ups, flips, proj, second, left_two, slope, right_one, first, late_from):
    rows, width = slope.shape
    _, hid_count, links, size, _ = first.shape
    count_in = ups[0][0].shape[1] // size
    group = hid_count // count_in
    rank = proj.shape[1]
    late = links - late_from
    shares = [[rows * n // 8 for n in link if n] for link in shares_of(BACK_SHARES, late)]
    pieces = [n for link in shares for n in link]
    in_specs = piece_specs(ups, flips, size)
    in_specs.append(pl.BlockSpec((rows, rank), lambda c, j: (0, 0)))
    in_specs += [
        pl.BlockSpec((None, None, None, size, size), lambda c, j, k=k: (0, c * group + j, k, 0, 0))
        for k in range(links)
    ]
    in_specs.append(pl.BlockSpec((None, size, rank), lambda c, j: (0, c * group + j, 0)))
    in_specs.append(pl.BlockSpec((rows, size), lambda c, j: (0, c * group + j)))
    in_specs.append(pl.BlockSpec((None, rank, group * size), lambda c, j: (0, 0, c)))
    in_specs += [
        pl.BlockSpec((None, group, None, size, size), lambda c, j, k=k: (0, c, k, 0, 0))
        for k in range(late_from, links)
    ]
    out_specs = [pl.BlockSpec((rows, size), lambda c, j: (0, c * group + j))]
    out_specs += [pl.BlockSpec((n, size), lambda c, j: (0, c)) for n in pieces]
    out_specs.append(pl.BlockSpec((rows, rank), lambda c, j: (0, 0)))
    out_shape = [jax.ShapeDtypeStruct((rows, width), BF16)]
    out_shape += [jax.ShapeDtypeStruct((n, count_in * size), BF16) for n in pieces]
    out_shape.append(jax.ShapeDtypeStruct((rows, rank), F32))
    return pl.pallas_call(
        functools.partial(
            hidden_kernel, [len(link) for link in ups], [len(link) for link in shares], group
        ),
        grid=(count_in, group),
        in_specs=in_specs,
        out_specs=out_specs,
        out_shape=out_shape,
        scratch_shapes=[
            pltpu.VMEM((rows, links * size + rank), BF16),
            pltpu.VMEM((rows, group * size), BF16),
        ],
        name="hidden_grad",
        **params(2),
    )(
        *[piece for link in ups for piece in link], proj, *[second] * links, left_two, slope, right_one, *[first] * late
    )


def near_kernel(near, group, hid, *refs):
    weights, refs = refs[0], refs[1:]
    far_weights, base, *far, total = refs
    kk = pl.program_id(1)
    term = nt(hid[...], wide([weights[g] for g in range(group)]))

    @pl.when(kk == 0)
    def _():
        total[...] = term
        other = nt(hid[...], wide([far_weights[g] for g in range(group)])).astype(BF16)
        for m, piece in enumerate(far):
            piece[...] = other[m * piece.shape[0] : (m + 1) * piece.shape[0]]

    @pl.when(kk > 0)
    def _():
        total[...] += term

    @pl.when(kk == near - 1)
    def _():
        base[...] = total[...]


def near_call(hidden, first, count_in, near):
    rows = hidden.shape[0]
    _, hid_count, links, size, _ = first.shape
    group = hid_count // count_in

    def mate(c, kk):
        return c ^ ((1 << kk) >> 1)

    width = count_in * size
    return pl.pallas_call(
        functools.partial(near_kernel, near, group),
        grid=(count_in, near),
        in_specs=[
            pl.BlockSpec((rows, group * size), lambda c, kk: (0, mate(c, kk))),
            pl.BlockSpec(
                (None, group, None, size, size), lambda c, kk: (0, mate(c, kk), kk, 0, 0)
            ),
            pl.BlockSpec((None, group, None, size, size), lambda c, kk: (0, c, near, 0, 0)),
        ],
        out_specs=[
            pl.BlockSpec((rows, size), lambda c, kk: (0, c)),
            *[pl.BlockSpec((rows // 2, size), lambda c, kk: (0, c))] * 2,
        ],
        out_shape=[
            jax.ShapeDtypeStruct((rows, width), F32),
            *[jax.ShapeDtypeStruct((rows // 2, width), BF16)] * 2,
        ],
        scratch_shapes=[pltpu.VMEM((rows, size), F32)],
        name="near_parts",
        **params(2),
    )(hidden, first, first)


def second_kernel(counts, group, has_proj, *refs):
    count = len(counts)
    ups, refs = taken(refs, counts)
    if has_proj:
        proj, act, _, out, left_two, turned = refs
    else:
        act, out, turned = refs
    k = pl.program_id(1)
    size = ups[0][0].shape[1]

    @pl.when(k == 0)
    def _():
        for g in range(group):
            turned[g * size : (g + 1) * size, :] = act[:, g * size : (g + 1) * size].T

    def store(pieces):
        up = jnp.concatenate([piece[...] for piece in pieces], axis=0)
        grads = nn(turned[...], up).astype(BF16)
        for g in range(group):
            out[g] = grads[g * size : (g + 1) * size]

    for n in range(count):
        pl.when(k == n)(lambda n=n: store(ups[n]))

    if has_proj:

        @pl.when(k == count - 1)
        def _():
            left_two[...] = nn(turned[...], proj[...]).astype(BF16)


def second_call(ups, flips, act, shape, start, proj=None, partial=None):
    count = len(ups)
    tokens = act.shape[0]
    _, hid_count, links, size, _ = shape
    count_in = ups[0][0].shape[1] // size
    group = hid_count // count_in
    has_proj = proj is not None
    in_specs = piece_specs(ups, flips, size)
    args = [piece for link in ups for piece in link]
    out_specs = [
        pl.BlockSpec((None, group, None, size, size), lambda c, k: (0, c, start + k, 0, 0))
    ]
    out_shape = [jax.ShapeDtypeStruct(shape, BF16)]
    aliases = {}
    if has_proj:
        rank = proj.shape[1]
        in_specs.append(pl.BlockSpec((tokens, rank), lambda c, k: (0, 0)))
        args.append(proj)
        out_specs.append(pl.BlockSpec((None, group * size, rank), lambda c, k: (0, c, 0)))
        out_shape.append(jax.ShapeDtypeStruct((1, hid_count * size, rank), BF16))
    in_specs.append(pl.BlockSpec((tokens, group * size), lambda c, k: (0, c)))
    args.append(act)
    if has_proj:
        in_specs.append(pl.BlockSpec(memory_space=pl.ANY))
        args.append(partial)
        aliases = {len(args) - 1: 0}
    return pl.pallas_call(
        functools.partial(second_kernel, [len(link) for link in ups], group, has_proj),
        grid=(count_in, count),
        in_specs=in_specs,
        out_specs=out_specs,
        out_shape=out_shape,
        scratch_shapes=[pltpu.VMEM((group * size, tokens), BF16)],
        input_output_aliases=aliases,
        name="second_late" if has_proj else "second_early",
        **params(2),
    )(*args)


def first_kernel(counts, *refs):
    links = len(counts)
    ins, refs = taken(refs, counts)
    proj, hid, out, right_one, in_all = refs
    size = hid.shape[1]

    @pl.when(pl.program_id(1) == 0)
    def _():
        for k in range(links):
            start = 0
            for piece in ins[k]:
                stop = start + piece.shape[0]
                in_all[k * size : (k + 1) * size, start:stop] = piece[...].T
                start = stop
        in_all[links * size :, :] = proj[...].T

    grads = nn(in_all[...], hid[...]).astype(BF16)
    for k in range(links):
        out[k] = grads[k * size : (k + 1) * size]
    right_one[...] = grads[links * size :]


def first_call(ins, flips, proj, hidden, shape):
    tokens, width = hidden.shape
    _, hid_count, links, size, _ = shape
    count_in = ins[0][0].shape[1] // size
    group = hid_count // count_in
    rank = proj.shape[1]
    in_specs = piece_specs(ins, flips, size)
    in_specs.append(pl.BlockSpec((tokens, rank), lambda c, j: (0, 0)))
    in_specs.append(pl.BlockSpec((tokens, size), lambda c, j: (0, c * group + j)))
    return pl.pallas_call(
        functools.partial(first_kernel, [len(link) for link in ins]),
        grid=(count_in, group),
        in_specs=in_specs,
        out_specs=[
            pl.BlockSpec(
                (None, None, links, size, size), lambda c, j: (0, c * group + j, 0, 0, 0)
            ),
            pl.BlockSpec((None, rank, size), lambda c, j: (0, 0, c * group + j)),
        ],
        out_shape=[
            jax.ShapeDtypeStruct(shape, BF16),
            jax.ShapeDtypeStruct((1, rank, width), BF16),
        ],
        scratch_shapes=[pltpu.VMEM((links * size + rank, tokens), BF16)],
        name="first_grad",
        **params(2),
    )(*[piece for link in ins for piece in link], proj, hidden)


def body(
    inputs, preact, handoff, first_blocks, second_blocks, left_one, right_one, left_two, right_two
):
    shape = first_blocks.shape
    links, size = shape[2], shape[-1]
    tokens, feats = inputs.shape[1:]
    count_in = feats // size
    near = count_in.bit_length()
    flips = [(1 << k) >> 1 if k < near else 0 for k in range(links)]
    spans = [slice(0, tokens // 2), slice(tokens // 2, tokens)]

    far_count = links - near - 1

    def half_sent(value):
        return [swapped(value, bit) for bit in reversed(range(1, far_count + 1))][::-1]

    ranks = left_one.shape[2]
    first_half, second_half = spans

    in_core = swapped(inputs[0], 0)
    in_one = half_sent(inputs[0, first_half])
    act, slope, proj_act = gate_call(preact, left_two, size)
    early = jnp.concatenate([nn(inputs[0], left_one[0]), proj_act], axis=1)

    upstream = after(shifted(handoff[0]), in_core, early, *in_one)
    up_core = swapped(upstream, 0)
    near_ups = [[upstream]] * near + [[up_core]]
    (second_part,) = second_call(near_ups, flips[: near + 1], act, shape, 0)
    up_shares = shares_of(UP_SHARES, far_count)
    sums, stage, far_ups = relay(
        [cut(upstream, shares) for shares in up_shares],
        jnp.concatenate([nt(upstream, right_two[0]), early], axis=1),
        lambda stage: [second_part],
    )
    proj_grad, proj_in, proj_act = jnp.split(sums, (ranks, 2 * ranks), axis=1)

    in_two = [
        swapped(after(inputs[0], far_ups[-1][1] if bit == far_count else stage)[second_half], bit)
        for bit in range(1, far_count + 1)
    ]
    hidden, *parts, back = hidden_call(
        near_ups + far_ups,
        flips,
        proj_grad,
        second_blocks,
        left_two,
        slope,
        right_one,
        first_blocks,
        near + 1,
    )
    in_sets = [[inputs[0]]] * near + [[in_core]] + [list(link) for link in zip(in_one, in_two)]
    back, *parts = lax.optimization_barrier((back, *parts, *in_two))[: 1 + len(parts)]
    found = []

    def work(stage):
        base, *beside = near_call(after(hidden, stage), first_blocks, count_in, near)
        second_grad, lefttwo_grad = second_call(
            far_ups, flips[near + 1 :], act, shape, near + 1, after(proj_grad, stage), second_part
        )
        first_grad, rightone_grad = first_call(
            in_sets, flips, after(proj_in, stage), hidden, shape
        )
        beside = jnp.concatenate([swapped(piece, 0) for piece in beside], axis=0)
        found.extend(
            [base, beside, first_grad, second_grad, rightone_grad, lefttwo_grad]
        )
        return [base, lefttwo_grad, rightone_grad]

    parts = iter(parts)
    back_links = [
        [next(parts) if share else None for share in shares]
        for shares in shares_of(BACK_SHARES, far_count)
    ]
    back_rank, _, far = relay(back_links, back, work)
    base, beside, first_grad, second_grad, rightone_grad, lefttwo_grad = found
    base = base + beside.astype(F32) + nt(back_rank, left_one[0])
    leftone_grad = nn(inputs[0].T, back_rank).astype(BF16)[None]
    righttwo_grad = nn(proj_act.T, upstream).astype(BF16)[None]
    total, leftone_grad, righttwo_grad = lax.optimization_barrier(
        (base, leftone_grad, righttwo_grad)
    )
    for link in far:
        total = total + jnp.concatenate(link, axis=0).astype(F32)
    input_grad = total.astype(BF16)[None]
    return (
        input_grad,
        first_grad,
        second_grad,
        leftone_grad,
        rightone_grad,
        lefttwo_grad,
        righttwo_grad,
    )


def solution(mesh):
    by_feature = P("section", None, "tensor")
    by_block = P("section", "tensor", None, None, None)
    by_row = P("section", "tensor", None)
    in_specs = (
        by_feature,
        by_feature,
        by_feature,
        by_block,
        by_block,
        by_row,
        by_feature,
        by_row,
        by_feature,
    )
    out_specs = (
        by_feature,
        by_block,
        by_block,
        by_row,
        by_feature,
        by_row,
        by_feature,
    )
    return jax.shard_map(body, mesh=mesh, in_specs=in_specs, out_specs=out_specs, check_vma=False)
```
